128 devices in a mesh: row: 16 (over z_lo, x, core), col: 8 (over z_hi, y).
Axes of the slice: x: 4, y: 4, z: 4 (z_hi: 2, z_lo: 2; z = z_hi * 2 + z_lo), core: 2. Of those that a mesh axis runs over, the one named last changes fastest.
Arguments:
- pair_input: bfloat16 [640, 640, 128], P('row', 'col'), may hold values from -6 to 6
- token_mask: int32 [640], replicated, may hold values from 0 to 1, as said below
- ln_gain: float32 [2, 128], replicated, may hold values from 0.1 to 1.9
- w_query: bfloat16 [2, 128, 128], replicated, may hold values from -24 to 24
- w_key: bfloat16 [2, 128, 128], replicated, may hold values from -0.5 to 0.5
- w_value: bfloat16 [2, 128, 128], replicated, may hold values from -0.5 to 0.5
- w_gate: bfloat16 [2, 128, 128], replicated, may hold values from -0.5 to 0.5
- w_bias: bfloat16 [2, 128, 4], replicated, may hold values from -1 to 1
- w_out: bfloat16 [2, 128, 128], replicated, may hold values from -0.5 to 0.5
Outputs:
- pair_out: bfloat16 [640, 640, 128], P('row', 'col')
The draws below stay inside these ranges and needn't reach their ends.
Inputs may be any that keep to these rules, and one draw needn't show every extreme that they name: `token_mask`: 0 marks a padded token and 1 a real one; at least one token is real and at least one is padded.
All inputs are finite; a program needn't handle non-finite values.
Results may differ from the reference program's by a relative error of at most 0.035.
The reference program's roundings to bfloat16 on the way (of `normed`, `queries`, `tri_bias`, `weights`, `attended` and `after_start`) count: a program that leaves them out, or rounds other values in their place, can miss the bound.
Values may be sent and summed in bfloat16 or wider, within the bound.
No kernel may reach another device: no remote copies, remote signals or barrier semaphores. Data moves between devices by JAX's collectives and lax.ppermute only.
A program may use at most 192 MiB of HBM per device.

```python
import jax
import jax.numpy as jnp
from jax import lax

C = 128
H = 4
HD = 32
N = 640


def draw_token_mask(key, part):
    key = jax.random.fold_in(key, 11)
    leading, second, third = jax.random.split(key, 3)
    kept_tokens = (jax.random.randint(leading, (N,), 0, 8) < 7).astype(jnp.int32)
    chosen = jax.random.randint(second, (), 0, N)
    dropped = (chosen + 1 + jax.random.randint(third, (), 0, N - 1)) % N
    positions = jnp.arange(N)
    kept_tokens = jnp.where(positions == chosen, 1, kept_tokens)
    kept_tokens = jnp.where(positions == dropped, 0, kept_tokens)
    return kept_tokens.astype(jnp.int32)


def draw_w_query(key, part):
    key = jax.random.fold_in(key, 5)
    base = jax.random.normal(key, (2, C, C), jnp.float32) * C ** (-0.5)
    return jnp.clip(base, -24.0, 24.0).astype(jnp.bfloat16)


def steps_of(stream_key, shape, shards, smallest, largest):
    gain, own = 1.0, jax.random.fold_in(stream_key, 6)
    for dim, shards_of in shards:
        steps = jnp.exp(jax.random.uniform(jax.random.fold_in(own, dim), (shards_of,), jnp.float32, smallest / len(shards), largest / len(shards)))
        gain = gain * jnp.repeat(steps, shape[dim] // shards_of).reshape([-1 if axis == dim else 1 for axis in range(len(shape))])
    return gain


def normal_values(rng, shape, scale, most, cuts=(), held_as=jnp.bfloat16):
    gain = steps_of(rng, shape, cuts, -0.22, 0.18) if cuts else 1.0
    entries = jax.random.normal(rng, shape, jnp.float32) * scale * gain
    return jnp.minimum(jnp.maximum(entries, -most), most).astype(held_as)


def setup_inputs(seed: int = 0) -> dict:
    keys = jax.random.split(jax.random.key(seed), 10)
    return {
        "pair_input": normal_values(keys[0], (N, N, C), 1.0, 6.0, ((0, 16), (1, 8))),
        "token_mask": draw_token_mask(jax.random.fold_in(keys[9], 71), 0),
        "ln_gain": jnp.clip(1.0 + 0.18 * jax.random.normal(keys[2], (2, C), jnp.float32), 0.1, 1.9),
        "w_query": draw_w_query(jax.random.fold_in(keys[9], 71), 0),
        "w_key": normal_values(keys[4], (2, C, C), C ** -0.5, 0.5),
        "w_value": normal_values(keys[5], (2, C, C), C ** -0.5, 0.5),
        "w_gate": normal_values(keys[6], (2, C, C), C ** -0.5, 0.5),
        "w_bias": normal_values(keys[7], (2, C, H), (C // 4) ** -0.5, 1.0),
        "w_out": normal_values(keys[8], (2, C, C), C ** -0.5, 0.5),
    }


epsilon = 1e-05
masked_score = -1e+30

def normalize(pair_block, gain_row):
    upcast = pair_block.astype(jnp.float32)
    centred = upcast - lax.optimization_barrier(jnp.mean(upcast, axis=-1, keepdims=True))
    variance = lax.optimization_barrier(jnp.mean(centred * centred, axis=-1, keepdims=True))
    return (centred * lax.rsqrt(variance + epsilon) * gain_row).astype(jnp.bfloat16)

def project(flattened, weight):
    return jnp.dot(flattened, weight, preferred_element_type=jnp.float32).astype(jnp.bfloat16)

def widened(array):
    return lax.optimization_barrier(array).astype(jnp.float32)

def starting_node(pair_input, token_mask, gain_row, w_query, w_key, w_value, w_gate, w_bias, w_out):
    extent = pair_input.shape[0]
    channels = pair_input.shape[2]
    normed = normalize(pair_input, gain_row)
    flattened = normed.reshape(-1, channels)
    head_shape = (extent, extent, H, HD)
    queries = project(flattened, w_query).reshape(head_shape)
    key_heads = project(flattened, w_key).reshape(head_shape)
    value_heads = project(flattened, w_value).reshape(head_shape)
    gating = jax.nn.sigmoid(jnp.dot(flattened, w_gate, preferred_element_type=jnp.float32)).reshape(head_shape)
    tri_bias = project(flattened, w_bias).reshape(extent, extent, H)
    bias_wide = widened(jnp.transpose(tri_bias, (0, 2, 1)))
    usable = token_mask > 0
    usable_float = usable.astype(jnp.float32)
    score_scale = HD ** (-0.5)

    def one_row(operands):
        row_queries, row_keys, row_values, row_gate = operands
        scores = jnp.einsum('jhd,khd->jhk', widened(row_queries), widened(row_keys)) * score_scale + bias_wide
        scores = jnp.where(usable, scores, masked_score)
        highest = lax.optimization_barrier(jnp.max(scores, axis=-1, keepdims=True))
        exponentials = jnp.exp(scores - highest) * usable_float
        totals = lax.optimization_barrier(jnp.sum(exponentials, axis=-1))
        weights = exponentials.astype(jnp.bfloat16)
        mixed = jnp.einsum('jhk,khd->jhd', widened(weights), widened(row_values))
        return (mixed / totals[..., None] * row_gate).astype(jnp.bfloat16)
    attended = lax.map(one_row, (queries, key_heads, value_heads, gating))
    update = jnp.dot(attended.reshape(-1, channels), w_out, preferred_element_type=jnp.float32)
    update = update.reshape(pair_input.shape)
    return (pair_input.astype(jnp.float32) + update).astype(jnp.bfloat16)

def reference(pair_input, token_mask, ln_gain, w_query, w_key, w_value, w_gate, w_bias, w_out):
    after_start = starting_node(pair_input, token_mask, ln_gain[0], w_query[0], w_key[0], w_value[0], w_gate[0], w_bias[0], w_out[0])
    flipped = jnp.swapaxes(after_start, 0, 1)
    after_end = starting_node(flipped, token_mask, ln_gain[1], w_query[1], w_key[1], w_value[1], w_gate[1], w_bias[1], w_out[1])
    return jnp.swapaxes(after_end, 0, 1)
```

```python
import functools

import jax
import jax.numpy as jnp
from jax import lax
from jax.experimental import pallas as pl
from jax.experimental.pallas import tpu as pltpu
from jax.sharding import PartitionSpec as P

H = 4
HD = 32
C = 128
N = 640
HALF = N // 2
PART = 40
OWN = 5

epsilon = 1e-05
masked_score = -1e30
LOG2E = 1.4426950408889634
SCALE = HD ** (-0.5) * LOG2E

SAME_CORE = [[core + 2 * place for place in range(8)] for core in range(2)]
PARTNER = [(place, place ^ 1) for place in range(16)]

CONTRACT_LAST = (((1,), (1,)), ((), ()))


def normalize(block, gain_row):
    upcast = block.astype(jnp.float32)
    centred = upcast - jnp.mean(upcast, axis=-1, keepdims=True)
    variance = jnp.mean(centred * centred, axis=-1, keepdims=True)
    return (centred * lax.rsqrt(variance + epsilon) * gain_row).astype(jnp.bfloat16)


def dot(left, right):
    return jnp.dot(left, right, preferred_element_type=jnp.float32)


def head_lanes(rows, head):
    lane = lax.broadcasted_iota(jnp.int32, (rows, C), 1)
    return (lane >= head * HD) & (lane < (head + 1) * HD)


def attend_row(queries_in, others_in, bias_s, gain, w_own, w_other, w_out):
    own = normalize(queries_in, gain)
    other = normalize(others_in, gain)
    own_all = dot(own, w_own)
    other_all = dot(other, w_other)
    queries = own_all[:, :C].astype(jnp.bfloat16).astype(jnp.float32) * SCALE
    gating = jax.nn.sigmoid(own_all[:, C : 2 * C])
    keys = jnp.concatenate([own_all[:, 2 * C : 3 * C], other_all[:, :C]], axis=0).astype(jnp.bfloat16)
    values = jnp.concatenate([own_all[:, 3 * C :], other_all[:, C:]], axis=0).astype(jnp.bfloat16)
    coarse = queries.astype(jnp.bfloat16)
    fine = (queries - coarse.astype(jnp.float32)).astype(jnp.bfloat16)
    both_keys = jnp.concatenate([keys, keys], axis=1)
    summed = None
    for head in range(H):
        lanes = head_lanes(HALF, head)
        zero = jnp.zeros((HALF, C), jnp.bfloat16)
        picked = jnp.concatenate([jnp.where(lanes, coarse, zero), jnp.where(lanes, fine, zero)], axis=1)
        scores = lax.dot_general(picked, both_keys, CONTRACT_LAST, preferred_element_type=jnp.float32)
        scores = scores + bias_s[head]
        highest = jnp.max(scores, axis=-1, keepdims=True)
        weights = jnp.exp2(scores - highest).astype(jnp.bfloat16)
        key_lanes = head_lanes(N, head)
        zeros = jnp.zeros((N, C), jnp.bfloat16)
        ones = jnp.ones((N, C), jnp.bfloat16)
        sources = jnp.concatenate([jnp.where(key_lanes, values, zeros), jnp.where(key_lanes, ones, zeros)], axis=1)
        mixed = dot(weights, sources)
        summed = mixed if summed is None else summed + mixed
    hidden = (summed[:, :C] / summed[:, C:] * gating).astype(jnp.bfloat16)
    return (queries_in.astype(jnp.float32) + dot(hidden, w_out)).astype(jnp.bfloat16)


def start_kernel(
    xa, xs, bias, mask, gain, w_own, w_other, w_out, next_gain, next_bias, out, tile, bias_s
):
    @pl.when(pl.program_id(0) == 0)
    def _():
        for head in range(H):
            for place in range(8):
                bias_s[head, place * PART : (place + 1) * PART, :] = (
                    bias[place, head].astype(jnp.float32) * LOG2E + mask[...]
                )

    for slot, source in enumerate((xa, xs)):
        after = attend_row(
            source[slot, 0], source[1 - slot, 0], bias_s, gain[...], w_own[...], w_other[...], w_out[...]
        )
        out[slot, 0] = after
        normed = normalize(after, next_gain[...])
        tile[slot, 0] = lax.dot_general(
            next_bias[...], normed, CONTRACT_LAST, preferred_element_type=jnp.float32
        )


def end_kernel(xa, xs, bias, mask, gain, w_own, w_other, w_out, out, bias_s, turned_s):
    @pl.when(pl.program_id(0) == 0)
    def _():
        row = lax.broadcasted_iota(jnp.int32, (HALF, HALF), 0)
        col = lax.broadcasted_iota(jnp.int32, (HALF, HALF), 1)
        identity = jnp.where(row == col, 1.0, 0.0).astype(jnp.bfloat16)
        for head in range(H):
            for side in range(2):
                for place in range(8):
                    first = side * HALF + place * PART
                    turned_s[first : first + PART, :] = bias[place, head, side].astype(jnp.float32)
            turned = lax.dot_general(
                identity,
                turned_s[...].astype(jnp.bfloat16),
                CONTRACT_LAST,
                preferred_element_type=jnp.float32,
            )
            bias_s[head] = turned * LOG2E + mask[...]

    for slot, source in enumerate((xa, xs)):
        out[slot, 0] = attend_row(
            source[slot, 0], source[1 - slot, 0], bias_s, gain[...], w_own[...], w_other[...], w_out[...]
        )


def whole(array):
    return pl.BlockSpec(array.shape, lambda step: (0,) * array.ndim)


def attend(xa, xs, bias, mask, gain, w_own, w_other, w_out, following):
    rows = pl.BlockSpec((2, 1, HALF, C), lambda step: (0, step, 0, 0))
    out_shape = [jax.ShapeDtypeStruct((2, OWN, HALF, C), jnp.bfloat16)]
    out_specs = [rows]
    scratch = [pltpu.VMEM((H, HALF, N), jnp.float32)]
    operands = [bias, mask, gain, w_own, w_other, w_out]
    if following is None:
        kernel = end_kernel
        scratch.append(pltpu.VMEM((N, HALF), jnp.float32))
    else:
        kernel = start_kernel
        operands += following
        out_shape.append(jax.ShapeDtypeStruct((2, OWN, 8, HALF), jnp.float32))
        out_specs.append(pl.BlockSpec((2, 1, 8, HALF), lambda step: (0, step, 0, 0)))
    return pl.pallas_call(
        kernel,
        grid=(OWN,),
        in_specs=[rows, rows] + [whole(member) for member in operands],
        out_specs=out_specs,
        out_shape=out_shape,
        scratch_shapes=scratch,
        compiler_params=pltpu.CompilerParams(vmem_limit_bytes=56 * 1024 * 1024),
    )(xa, xs, *operands)


def by_core(array, axis, core):
    return jnp.where(core == 1, jnp.flip(array, axis), array)


def gather(array, axis, groups=None):
    copies = jnp.broadcast_to(array[None], (8,) + array.shape)
    return lax.all_to_all(copies, axis, 0, 0, axis_index_groups=groups)


def body(pair_input, token_mask, ln_gain, w_query, w_key, w_value, w_gate, w_bias, w_out):
    core = lax.axis_index("row") % 2
    mask_row = jnp.where(token_mask > 0, 0.0, masked_score).astype(jnp.float32)
    mask_row = by_core(mask_row.reshape(8, 2, PART), 1, core).transpose(1, 0, 2).reshape(1, N)
    w_own = jnp.concatenate([w_query, w_gate, w_key, w_value], axis=2)
    w_other = jnp.concatenate([w_key, w_value], axis=2)
    next_bias = jnp.pad(w_bias[1].T, ((0, 4), (0, 0)))

    halves = by_core(pair_input.reshape(PART, 2, PART, C), 1, core)
    normed = normalize(halves, ln_gain[0])
    tile = jnp.einsum("jskc,ch->hjsk", normed, w_bias[0], preferred_element_type=jnp.float32)
    tile = gather(tile.astype(jnp.bfloat16), "col")
    tile = tile.transpose(1, 2, 3, 0, 4).reshape(H, PART, N)
    bias = gather(tile, "row", SAME_CORE)
    xa = lax.all_to_all(halves.transpose(1, 0, 2, 3), "col", 1, 2, tiled=True)
    xs = lax.ppermute(xa, "row", PARTNER)
    after, tile = attend(
        xa,
        xs,
        bias,
        mask_row,
        ln_gain[0:1],
        w_own[0],
        w_other[0],
        w_out[0],
        [ln_gain[1:2], next_bias],
    )

    tile = tile[:, :, :H].transpose(2, 0, 1, 3).astype(jnp.bfloat16)
    tile = gather(tile, "col").transpose(1, 2, 0, 3, 4).reshape(H, 2, PART, HALF)
    bias = gather(tile, "row", SAME_CORE)
    block = lax.all_to_all(after.reshape(2, OWN, 8, PART, C), "col", 2, 1, tiled=True)
    block = block.reshape(2, PART, PART, C).transpose(0, 2, 1, 3)
    pieces = block.reshape(2, 8, OWN, PART, C)
    xa = lax.all_to_all(pieces, "row", 1, 3, axis_index_groups=SAME_CORE, tiled=True)
    xa = xa.reshape(2, OWN, HALF, C)
    xs = lax.ppermute(xa, "row", PARTNER)
    (after,) = attend(
        xa, xs, bias, mask_row, ln_gain[1:2], w_own[1], w_other[1], w_out[1], None
    )
    pieces = after.reshape(2, OWN, 8, PART, C)
    block = lax.all_to_all(pieces, "row", 2, 1, axis_index_groups=SAME_CORE, tiled=True)
    block = by_core(block.reshape(2, PART, PART, C), 0, core)
    return block.transpose(2, 0, 1, 3).reshape(PART, 2 * PART, C)


def solution(mesh):
    placed = (P("row", "col", None), P(), P(), P(), P(), P(), P(), P(), P())
    return jax.shard_map(
        body, mesh=mesh, in_specs=placed, out_specs=P("row", "col", None), check_vma=False
    )
```

```python
import functools

import jax
import jax.numpy as jnp
from jax import lax
from jax.experimental import pallas as pl
from jax.experimental.pallas import tpu as pltpu
from jax.sharding import PartitionSpec as P

H = 4
HD = 32
C = 128
N = 640
HALF = N // 2
PART = 40
OWN = 5

epsilon = 1e-05
masked_score = -1e30
LOG2E = 1.4426950408889634
SCALE = HD ** (-0.5) * LOG2E

SAME_CORE = [[core + 2 * place for place in range(8)] for core in range(2)]
CORE_PLANES = [
    [(core + 2 * place) * 8 + column for place in range(8) for column in range(8)]
    for core in range(2)
]
PARTNER = [(place, place ^ 1) for place in range(16)]

CHUNKS = N // C
VMEM = 30 * 1024 * 1024
CONTRACT_LAST = (((1,), (1,)), ((), ()))


def normalize(upcast, gain_row):
    centred = upcast - jnp.mean(upcast, axis=-1, keepdims=True)
    variance = jnp.mean(centred * centred, axis=-1, keepdims=True)
    return (centred * lax.rsqrt(variance + epsilon) * gain_row).astype(jnp.bfloat16)


def dot(left, right):
    return jnp.dot(left, right, preferred_element_type=jnp.float32)


def head_lanes(rows, head):
    lane = lax.broadcasted_iota(jnp.int32, (rows, C), 1)
    return (lane >= head * HD) & (lane < (head + 1) * HD)


def attend_row(queries_in, others_in, bias_s, gain, w_query, w_key, w_value, w_gate, w_out):
    own = normalize(queries_in, gain)
    other = normalize(others_in, gain)
    own_all = dot(own, jnp.concatenate([w_query, w_gate, w_key, w_value], axis=1))
    other_all = dot(other, jnp.concatenate([w_key, w_value], axis=1))
    queries = own_all[:, :C].astype(jnp.bfloat16).astype(jnp.float32) * SCALE
    gating = jax.nn.sigmoid(own_all[:, C : 2 * C])
    keys = jnp.concatenate([own_all[:, 2 * C : 3 * C], other_all[:, :C]], axis=0).astype(jnp.bfloat16)
    values = jnp.concatenate([own_all[:, 3 * C :], other_all[:, C:]], axis=0).astype(jnp.bfloat16)
    coarse = queries.astype(jnp.bfloat16)
    fine = (queries - coarse.astype(jnp.float32)).astype(jnp.bfloat16)
    both_queries = jnp.concatenate([coarse, fine], axis=1)
    zeros = jnp.zeros((N, C), jnp.bfloat16)
    ones = jnp.ones((N, C), jnp.bfloat16)
    head_keys, head_sources = [], []
    for head in range(H):
        lanes = head_lanes(N, head)
        picked = jnp.where(lanes, keys, zeros)
        head_keys.append(jnp.concatenate([picked, picked], axis=1))
        head_sources.append(
            jnp.concatenate([jnp.where(lanes, values, zeros), jnp.where(lanes, ones, zeros)], axis=1)
        )
    all_scores = lax.dot_general(
        both_queries,
        jnp.concatenate(head_keys, axis=0),
        CONTRACT_LAST,
        preferred_element_type=jnp.float32,
    )
    head_weights = []
    for head in range(H):
        scores = all_scores[:, head * N : (head + 1) * N] + bias_s[head]
        highest = jnp.max(scores, axis=-1, keepdims=True)
        head_weights.append(jnp.exp2(scores - highest).astype(jnp.bfloat16))
    summed = dot(jnp.concatenate(head_weights, axis=1), jnp.concatenate(head_sources, axis=0))
    hidden = (summed[:, :C] / summed[:, C:] * gating).astype(jnp.bfloat16)
    return (queries_in + dot(hidden, w_out)).astype(jnp.bfloat16).astype(jnp.float32)


def start_kernel(own_q, own_o, far_q, far_o, mask, gain, next_bias, *rest):
    weights, bias = rest[:2]
    out, tile, bias_s = rest[2:]

    @pl.when(pl.program_id(0) == 0)
    def _():
        for place in range(8):
            for head in range(H):
                for part in range(CHUNKS):
                    lanes = slice(part * C, (part + 1) * C)
                    bias_s[head, place * PART : (place + 1) * PART, lanes] = (
                        bias[place, head, part].astype(jnp.float32) * LOG2E + mask[:, lanes]
                    )

    for slot, (queries, others) in enumerate(((own_q, own_o), (far_q, far_o))):
        after = attend_row(
            merged(queries), merged(others), bias_s, gain[0:1], *(weights[position] for position in range(5))
        )
        out[:, 0, slot] = after.reshape(8, PART, C).astype(jnp.bfloat16)
        normed = normalize(after, gain[1:2])
        tile[slot, 0] = lax.dot_general(
            next_bias[1], normed, CONTRACT_LAST, preferred_element_type=jnp.float32
        )


def end_kernel(own_q, own_o, far_q, far_o, mask, gain, *rest):
    weights, bias = rest[:2]
    out, bias_s, turned_s = rest[2:]

    @pl.when(pl.program_id(0) == 0)
    def _():
        row = lax.broadcasted_iota(jnp.int32, (HALF, 2 * HALF), 0)
        col = lax.broadcasted_iota(jnp.int32, (HALF, 2 * HALF), 1)
        for pair in range(2):
            for place in range(8):
                for side in range(2):
                    first = side * HALF + place * PART
                    for part in range(CHUNKS):
                        turned_s[pair, first : first + PART, part * C : (part + 1) * C] = bias[
                            place, pair, side, part
                        ].astype(jnp.float32)
        for head in range(H):
            chosen = jnp.where(row + (head % 2) * HALF == col, 1.0, 0.0).astype(jnp.bfloat16)
            turned = lax.dot_general(
                chosen,
                turned_s[head // 2].astype(jnp.bfloat16),
                CONTRACT_LAST,
                preferred_element_type=jnp.float32,
            )
            bias_s[head] = turned * LOG2E + mask[...]

    for slot, (queries, others) in enumerate(((own_q, own_o), (far_q, far_o))):
        after = attend_row(
            merged(queries), merged(others), bias_s, gain[1:2], *(weights[position] for position in range(5))
        )
        out[:, 0, slot] = after.reshape(8, PART, C).astype(jnp.bfloat16)


def merged(block):
    return block[...].astype(jnp.float32).reshape(HALF, C)


def tile_kernel(block, gain, head_bias, *rest):
    weights, (tile, stacked) = rest[:5], rest[5:]

    @pl.when(pl.program_id(0) == 0)
    def _():
        for position, weight in enumerate(weights):
            stacked[:, position] = weight[...]

    tokens = block[...].astype(jnp.float32).reshape(8 * 2 * PART, C)
    normed = normalize(tokens, gain[0:1])
    tile[...] = lax.dot_general(
        head_bias[0], normed, CONTRACT_LAST, preferred_element_type=jnp.float32
    )


def whole(array):
    return pl.BlockSpec(array.shape, lambda *_: (0,) * array.ndim)


def attend(section, xa, xs, mask, gain, next_bias, weights, bias):
    first = pl.BlockSpec((8, None, PART, C), lambda step: (0, step, 0, 0))
    second = pl.BlockSpec((8, None, PART, C), lambda step: (0, OWN + step, 0, 0))
    weight = pl.BlockSpec((None, 5, C, C), lambda step: (section, 0, 0, 0))
    out_shape = [jax.ShapeDtypeStruct((8, OWN, 2, PART, C), jnp.bfloat16)]
    out_specs = [pl.BlockSpec((8, 1, 2, PART, C), lambda step: (0, step, 0, 0, 0))]
    scratch = [pltpu.VMEM((H, HALF, N), jnp.float32)]
    shared = [mask, gain]
    if section == 0:
        shared.append(next_bias)
        out_shape.append(jax.ShapeDtypeStruct((2, OWN, 8, HALF), jnp.float32))
        out_specs.append(pl.BlockSpec((2, 1, 8, HALF), lambda step: (0, step, 0, 0)))
    else:
        scratch.append(pltpu.VMEM((2, N, 2 * HALF), jnp.float32))
    return pl.pallas_call(
        (start_kernel, end_kernel)[section],
        grid=(OWN,),
        in_specs=[first, second, second, first]
        + [whole(member) for member in shared]
        + [weight, whole(bias)],
        out_specs=out_specs,
        scratch_shapes=scratch,
        out_shape=out_shape,
        compiler_params=pltpu.CompilerParams(vmem_limit_bytes=VMEM),
        cost_estimate=pl.CostEstimate(
            flops=8_000_000_000, bytes_accessed=6_000_000, transcendentals=8_000_000
        ),
        name=("start_node", "end_node")[section],
    )(xa, xa, xs, xs, *shared, weights, bias)


def by_core(array, axis, core):
    return jnp.where(core == 1, jnp.flip(array, axis), array)


def to_columns(array):
    flat = array.reshape(8, -1, C)
    return lax.all_to_all(flat, "col", 0, 0, tiled=True).reshape(array.shape)


def to_rows(array):
    flat = array.reshape(8, -1, C)
    flat = lax.all_to_all(flat, "row", 0, 0, axis_index_groups=SAME_CORE, tiled=True)
    return flat.reshape(array.shape)


def to_all(array):
    return lax.all_to_all(array, ("row", "col"), 0, 0, axis_index_groups=CORE_PLANES, tiled=True)


def copies(array):
    return jnp.broadcast_to(array[None], (8,) + array.shape)


def body(pair_input, token_mask, ln_gain, w_query, w_key, w_value, w_gate, w_bias, w_out):
    core = lax.axis_index("row") % 2
    mask_row = jnp.where(token_mask > 0, 0.0, masked_score).astype(jnp.float32)
    mask_row = by_core(mask_row.reshape(8, 2, PART), 1, core).transpose(1, 0, 2).reshape(1, N)
    head_bias = jnp.pad(w_bias.transpose(0, 2, 1), ((0, 0), (0, 4), (0, 0)))
    weights = [w_query, w_key, w_value, w_gate, w_out]

    tile, weights = pl.pallas_call(
        tile_kernel,
        grid=(5,),
        in_specs=[
            pl.BlockSpec((8, 2 * PART, C), lambda step: (step, 0, 0)),
            whole(ln_gain),
            whole(head_bias),
        ]
        + [whole(weight) for weight in weights],
        out_specs=[
            pl.BlockSpec((8, 16 * PART), lambda step: (0, step)),
            pl.BlockSpec((2, 5, C, C), lambda step: (0, 0, 0, 0)),
        ],
        out_shape=[
            jax.ShapeDtypeStruct((8, 2 * PART * PART), jnp.float32),
            jax.ShapeDtypeStruct((2, 5, C, C), jnp.bfloat16),
        ],
        name="bias_tile",
    )(pair_input, ln_gain, head_bias, *weights)
    tile = by_core(tile[:H].reshape(H, PART, 2, PART), 2, core).astype(jnp.bfloat16)
    tile = jnp.pad(
        tile.transpose(1, 0, 2, 3).reshape(PART, HALF), ((0, 0), (0, 3 * C - HALF))
    )
    tile = tile.reshape(PART, 3, C).transpose(1, 0, 2)
    halves = by_core(pair_input.reshape(8, OWN, 2, PART, C), 2, core)
    halves = halves.transpose(0, 2, 1, 3, 4).reshape(8, 2 * OWN, PART, C)
    xa = to_columns(jnp.concatenate([halves, copies(tile)], axis=1))
    xs = lax.ppermute(xa, "row", PARTNER)
    tile = xa[:, 2 * OWN :].transpose(0, 2, 1, 3).reshape(8, PART, 3 * C)[..., :HALF]
    tile = tile.reshape(8, PART, H, 2, PART).transpose(2, 1, 3, 0, 4).reshape(H, PART, N)
    tile = tile.reshape(H, PART, CHUNKS, C).transpose(0, 2, 1, 3)
    tile, xs = lax.optimization_barrier((tile, xs))
    bias = to_rows(copies(tile))
    after, tile = attend(0, xa, xs, mask_row, ln_gain, head_bias, weights, bias)

    sent = after.reshape(8, OWN, 2, 8, OWN, C).transpose(3, 0, 2, 4, 1, 5)
    tile = tile[:, :, :H].astype(jnp.bfloat16).transpose(0, 1, 2, 3).reshape(2 * OWN, 2 * CHUNKS, C)
    tile = jnp.broadcast_to(
        tile.transpose(1, 0, 2).reshape(1, 100, C), (64, 100, C)
    )
    got = to_all(jnp.concatenate([sent.reshape(64, 2 * OWN * OWN, C), tile], axis=1))
    xa = got[:, : 2 * OWN * OWN].reshape(8, 8, 2 * OWN, OWN, C)
    xa = xa.transpose(0, 2, 1, 3, 4).reshape(8, 2 * OWN, PART, C)
    xs = lax.ppermute(xa, "row", PARTNER)
    bias = got[:, 2 * OWN * OWN :].reshape(8, 8, 2, CHUNKS, 2, OWN, C)
    bias = bias.transpose(0, 2, 4, 3, 1, 5, 6).reshape(8, 2, 2, CHUNKS, PART, C)
    (after,) = attend(1, xa, xs, mask_row, ln_gain, None, weights, bias)
    block = by_core(to_rows(after), 2, core)
    return block.transpose(3, 2, 0, 1, 4).reshape(PART, 2 * PART, C)


def solution(mesh):
    placed = (P("row", "col", None), P(), P(), P(), P(), P(), P(), P(), P())
    return jax.shard_map(
        body, mesh=mesh, in_specs=placed, out_specs=P("row", "col", None), check_vma=False
    )
```

```python
import functools

import jax
import jax.numpy as jnp
from jax import lax
from jax.experimental import pallas as pl
from jax.experimental.pallas import tpu as pltpu
from jax.sharding import PartitionSpec as P

H = 4
HD = 32
C = 128
N = 640
HALF = N // 2
PART = 40
OWN = 5

epsilon = 1e-05
masked_score = -1e30
LOG2E = 1.4426950408889634
SCALE = HD ** (-0.5) * LOG2E

SAME_CORE = [[core + 2 * place for place in range(8)] for core in range(2)]
CORE_PLANES = [
    [(core + 2 * place) * 8 + column for place in range(8) for column in range(8)]
    for core in range(2)
]
PARTNER = [(place, place ^ 1) for place in range(16)]

CHUNKS = N // C
VMEM = 30 * 1024 * 1024
CONTRACT_LAST = (((1,), (1,)), ((), ()))


def normalize(upcast, gain_row):
    centred = upcast - jnp.mean(upcast, axis=-1, keepdims=True)
    variance = jnp.mean(centred * centred, axis=-1, keepdims=True)
    return (centred * lax.rsqrt(variance + epsilon) * gain_row).astype(jnp.bfloat16)


def dot(left, right):
    return jnp.dot(left, right, preferred_element_type=jnp.float32)


def head_lanes(head):
    lane = lax.broadcasted_iota(jnp.int32, (1, C), 1)
    return jnp.where((lane >= head * HD) & (lane < (head + 1) * HD), 1.0, 0.0).astype(jnp.bfloat16)


def prepare(queries_in, others_in, gain, w_query, w_key, w_value, w_gate):
    own = normalize(queries_in, gain)
    other = normalize(others_in, gain)
    own_all = dot(own, jnp.concatenate([w_query, w_gate, w_key, w_value], axis=1))
    other_all = dot(other, jnp.concatenate([w_key, w_value], axis=1))
    queries = own_all[:, :C].astype(jnp.bfloat16).astype(jnp.float32) * SCALE
    gating = jax.nn.sigmoid(own_all[:, C : 2 * C])
    keys = jnp.concatenate([own_all[:, 2 * C : 3 * C], other_all[:, :C]], axis=0).astype(jnp.bfloat16)
    values = jnp.concatenate([own_all[:, 3 * C :], other_all[:, C:]], axis=0).astype(jnp.bfloat16)
    coarse = queries.astype(jnp.bfloat16)
    fine = (queries - coarse.astype(jnp.float32)).astype(jnp.bfloat16)
    both_queries = jnp.concatenate([coarse, fine], axis=1)
    head_keys, head_sources = [], []
    for head in range(H):
        lanes = head_lanes(head)
        picked = keys * lanes
        head_keys.append(jnp.concatenate([picked, picked], axis=1))
        head_sources.append(
            jnp.concatenate([values * lanes, jnp.broadcast_to(lanes, (N, C))], axis=1)
        )
    return both_queries, gating, head_keys, head_sources


def score(both_queries, head_keys):
    return lax.dot_general(
        both_queries, head_keys, CONTRACT_LAST, preferred_element_type=jnp.float32
    )


def softmax(scores, bias):
    scores = scores + bias
    highest = jnp.max(scores, axis=-1, keepdims=True)
    return jnp.exp2(scores - highest).astype(jnp.bfloat16)


def mix(head_weights, head_sources):
    return dot(jnp.concatenate(head_weights, axis=1), jnp.concatenate(head_sources, axis=0))


def finish(queries_in, summed, gating, w_out):
    hidden = (summed[:, :C] / summed[:, C:] * gating).astype(jnp.bfloat16)
    return (queries_in + dot(hidden, w_out)).astype(jnp.bfloat16).astype(jnp.float32)


def attend_rows(rows, bias_s, gain, w_query, w_key, w_value, w_gate, w_out):
    pre = [prepare(q, o, gain, w_query, w_key, w_value, w_gate) for q, o in rows]
    scores = [score(p[0], jnp.concatenate(p[2], axis=0)) for p in pre]
    summed = []
    for p, sc in zip(pre, scores):
        weights = [softmax(sc[:, h * N : (h + 1) * N], bias_s[h]) for h in range(H)]
        summed.append(mix(weights, p[3]))
    return [finish(q, m, p[1], w_out) for (q, o), m, p in zip(rows, summed, pre)]


def start_kernel(own_q, own_o, far_q, far_o, mask, gain, next_bias, *rest):
    weights, bias = rest[:2]
    out, tile, bias_s = rest[2:]

    @pl.when(pl.program_id(0) == 0)
    def _():
        for place in range(8):
            for head in range(H):
                for part in range(CHUNKS):
                    lanes = slice(part * C, (part + 1) * C)
                    bias_s[head, place * PART : (place + 1) * PART, lanes] = (
                        bias[place, head, part].astype(jnp.float32) * LOG2E + mask[:, lanes]
                    )

    afters = attend_rows(
        ((merged(own_q), merged(own_o)), (merged(far_q), merged(far_o))),
        bias_s,
        gain[0:1],
        *(weights[position] for position in range(5)),
    )
    for slot in range(2):
        after = afters[slot]
        out[:, 0, slot] = after.reshape(8, PART, C).astype(jnp.bfloat16)
        normed = normalize(after, gain[1:2])
        tile[slot, 0] = lax.dot_general(
            next_bias[1], normed, CONTRACT_LAST, preferred_element_type=jnp.float32
        )


def end_kernel(own_q, own_o, far_q, far_o, mask, gain, *rest):
    weights, bias = rest[:2]
    out, bias_s = rest[2:]

    @pl.when(pl.program_id(0) == 0)
    def _():
        row = lax.broadcasted_iota(jnp.int32, (HALF, HALF), 0)
        col = lax.broadcasted_iota(jnp.int32, (HALF, HALF), 1)
        identity = jnp.where(row == col, 1.0, 0.0).astype(jnp.bfloat16)
        for head in range(H):
            first = (head % 2) * HALF
            turned = lax.dot_general(
                identity,
                bias[head // 2, :, first : first + HALF],
                CONTRACT_LAST,
                preferred_element_type=jnp.float32,
            )
            bias_s[head] = turned * LOG2E + mask[...]

    afters = attend_rows(
        ((merged(own_q), merged(own_o)), (merged(far_q), merged(far_o))),
        bias_s,
        gain[1:2],
        *(weights[position] for position in range(5)),
    )
    for slot in range(2):
        after = afters[slot]
        out[:, 0, slot] = after.reshape(8, PART, C).astype(jnp.bfloat16)


def merged(block):
    return block[...].astype(jnp.float32).reshape(HALF, C)


def tile_kernel(block, gain, head_bias, *rest):
    weights, (tile, stacked) = rest[:5], rest[5:]

    @pl.when(pl.program_id(0) == 0)
    def _():
        for position, weight in enumerate(weights):
            stacked[:, position] = weight[...]

    tokens = block[...].astype(jnp.float32).reshape(8 * 2 * PART, C)
    normed = normalize(tokens, gain[0:1])
    tile[...] = lax.dot_general(
        head_bias[0], normed, CONTRACT_LAST, preferred_element_type=jnp.float32
    )


def whole(array):
    return pl.BlockSpec(array.shape, lambda *_: (0,) * array.ndim)


def attend(section, xa, xs, mask, gain, next_bias, weights, bias):
    first = pl.BlockSpec((8, None, PART, C), lambda step: (0, step, 0, 0))
    second = pl.BlockSpec((8, None, PART, C), lambda step: (0, OWN + step, 0, 0))
    weight = pl.BlockSpec((None, 5, C, C), lambda step: (section, 0, 0, 0))
    out_shape = [jax.ShapeDtypeStruct((8, OWN, 2, PART, C), jnp.bfloat16)]
    out_specs = [pl.BlockSpec((8, 1, 2, PART, C), lambda step: (0, step, 0, 0, 0))]
    scratch = [pltpu.VMEM((H, HALF, N), jnp.float32)]
    shared = [mask, gain]
    if section == 0:
        shared.append(next_bias)
        out_shape.append(jax.ShapeDtypeStruct((2, OWN, 8, HALF), jnp.float32))
        out_specs.append(pl.BlockSpec((2, 1, 8, HALF), lambda step: (0, step, 0, 0)))
    return pl.pallas_call(
        (start_kernel, end_kernel)[section],
        grid=(OWN,),
        in_specs=[first, second, second, first]
        + [whole(member) for member in shared]
        + [weight, whole(bias)],
        out_specs=out_specs,
        scratch_shapes=scratch,
        out_shape=out_shape,
        compiler_params=pltpu.CompilerParams(vmem_limit_bytes=VMEM),
        cost_estimate=pl.CostEstimate(
            flops=8_000_000_000, bytes_accessed=6_000_000, transcendentals=8_000_000
        ),
        name=("start_node", "end_node")[section],
    )(xa, xa, xs, xs, *shared, weights, bias)


def by_core(array, axis, core):
    return jnp.where(core == 1, jnp.flip(array, axis), array)


def to_columns(array):
    flat = array.reshape(8, -1, C)
    return lax.all_to_all(flat, "col", 0, 0, tiled=True).reshape(array.shape)


def to_rows(array):
    flat = array.reshape(8, -1, C)
    flat = lax.all_to_all(flat, "row", 0, 0, axis_index_groups=SAME_CORE, tiled=True)
    return flat.reshape(array.shape)


def to_all(array):
    return lax.all_to_all(array, ("row", "col"), 0, 0, axis_index_groups=CORE_PLANES, tiled=True)


def copies(array):
    return jnp.broadcast_to(array[None], (8,) + array.shape)


def body(pair_input, token_mask, ln_gain, w_query, w_key, w_value, w_gate, w_bias, w_out):
    core = lax.axis_index("row") % 2
    mask_row = jnp.where(token_mask > 0, 0.0, masked_score).astype(jnp.float32)
    mask_row = by_core(mask_row.reshape(8, 2, PART), 1, core).transpose(1, 0, 2).reshape(1, N)
    head_bias = jnp.pad(w_bias.transpose(0, 2, 1), ((0, 0), (0, 4), (0, 0)))
    weights = [w_query, w_key, w_value, w_gate, w_out]

    tile, weights = pl.pallas_call(
        tile_kernel,
        grid=(5,),
        in_specs=[
            pl.BlockSpec((8, 2 * PART, C), lambda step: (step, 0, 0)),
            whole(ln_gain),
            whole(head_bias),
        ]
        + [whole(weight) for weight in weights],
        out_specs=[
            pl.BlockSpec((8, 16 * PART), lambda step: (0, step)),
            pl.BlockSpec((2, 5, C, C), lambda step: (0, 0, 0, 0)),
        ],
        out_shape=[
            jax.ShapeDtypeStruct((8, 2 * PART * PART), jnp.float32),
            jax.ShapeDtypeStruct((2, 5, C, C), jnp.bfloat16),
        ],
        name="bias_tile",
    )(pair_input, ln_gain, head_bias, *weights)
    tile = by_core(tile[:H].reshape(H, PART, 2, PART), 2, core).astype(jnp.bfloat16)
    tile = jnp.pad(
        tile.transpose(1, 0, 2, 3).reshape(PART, HALF), ((0, 0), (0, 3 * C - HALF))
    )
    tile = tile.reshape(PART, 3, C).transpose(1, 0, 2)
    halves = by_core(pair_input.reshape(8, OWN, 2, PART, C), 2, core)
    halves = halves.transpose(0, 2, 1, 3, 4).reshape(8, 2 * OWN, PART, C)
    xa = to_columns(jnp.concatenate([halves, copies(tile)], axis=1))
    xs = lax.ppermute(xa, "row", PARTNER)
    tile = xa[:, 2 * OWN :].transpose(0, 2, 1, 3).reshape(8, PART, 3 * C)[..., :HALF]
    tile = tile.reshape(8, PART, H, 2, PART).transpose(2, 1, 3, 0, 4).reshape(H, PART, N)
    tile = tile.reshape(H, PART, CHUNKS, C).transpose(0, 2, 1, 3)
    tile, xs = lax.optimization_barrier((tile, xs))
    bias = to_rows(copies(tile))
    after, tile = attend(0, xa, xs, mask_row, ln_gain, head_bias, weights, bias)

    sent = after.reshape(8, OWN, 2, 8, OWN, C).transpose(3, 0, 2, 4, 1, 5)
    tile = tile[:, :, :H].astype(jnp.bfloat16).transpose(0, 1, 2, 3).reshape(2 * OWN, 2 * CHUNKS, C)
    tile = jnp.broadcast_to(
        tile.transpose(1, 0, 2).reshape(1, 100, C), (64, 100, C)
    )
    got = to_all(jnp.concatenate([sent.reshape(64, 2 * OWN * OWN, C), tile], axis=1))
    xa = got[:, : 2 * OWN * OWN].reshape(8, 8, 2 * OWN, OWN, C)
    xa = xa.transpose(0, 2, 1, 3, 4).reshape(8, 2 * OWN, PART, C)
    xs = lax.ppermute(xa, "row", PARTNER)
    bias = got[:, 2 * OWN * OWN :].reshape(8, 8, 2, CHUNKS, 2, OWN, C)
    bias = bias.transpose(2, 4, 0, 1, 5, 3, 6).reshape(2, N, N)
    (after,) = attend(1, xa, xs, mask_row, ln_gain, None, weights, bias)
    block = by_core(to_rows(after), 2, core)
    return block.transpose(3, 2, 0, 1, 4).reshape(PART, 2 * PART, C)


def solution(mesh):
    placed = (P("row", "col", None), P(), P(), P(), P(), P(), P(), P(), P())
    return jax.shard_map(
        body, mesh=mesh, in_specs=placed, out_specs=P("row", "col", None), check_vma=False
    )
```

```python
import functools

import jax
import jax.numpy as jnp
from jax import lax
from jax.experimental import pallas as pl
from jax.experimental.pallas import tpu as pltpu
from jax.sharding import PartitionSpec as P

H = 4
HD = 32
C = 128
N = 640
HALF = N // 2
PART = 40
OWN = 5

epsilon = 1e-05
masked_score = -1e30
LOG2E = 1.4426950408889634
SCALE = HD ** (-0.5) * LOG2E

SAME_CORE = [[core + 2 * place for place in range(8)] for core in range(2)]
CORE_PLANES = [
    [(core + 2 * place) * 8 + column for place in range(8) for column in range(8)]
    for core in range(2)
]
PARTNER = [(place, place ^ 1) for place in range(16)]

CHUNKS = N // C
VMEM = 30 * 1024 * 1024
CONTRACT_LAST = (((1,), (1,)), ((), ()))


def normalize(upcast, gain_row):
    centred = upcast - jnp.mean(upcast, axis=-1, keepdims=True)
    variance = jnp.mean(centred * centred, axis=-1, keepdims=True)
    return (centred * lax.rsqrt(variance + epsilon) * gain_row).astype(jnp.bfloat16)


def dot(left, right):
    return jnp.dot(left, right, preferred_element_type=jnp.float32)


def head_lanes(rows, head):
    lane = lax.broadcasted_iota(jnp.int32, (rows, C), 1)
    return (lane >= head * HD) & (lane < (head + 1) * HD)


def prepare(queries_in, others_in, gain, w_query, w_key, w_value, w_gate):
    own = normalize(queries_in, gain)
    other = normalize(others_in, gain)
    own_all = dot(own, jnp.concatenate([w_query, w_gate, w_key, w_value], axis=1))
    other_all = dot(other, jnp.concatenate([w_key, w_value], axis=1))
    queries = own_all[:, :C].astype(jnp.bfloat16).astype(jnp.float32) * SCALE
    gating = jax.nn.sigmoid(own_all[:, C : 2 * C])
    keys = jnp.concatenate([own_all[:, 2 * C : 3 * C], other_all[:, :C]], axis=0).astype(jnp.bfloat16)
    values = jnp.concatenate([own_all[:, 3 * C :], other_all[:, C:]], axis=0).astype(jnp.bfloat16)
    coarse = queries.astype(jnp.bfloat16)
    fine = (queries - coarse.astype(jnp.float32)).astype(jnp.bfloat16)
    both_queries = jnp.concatenate([coarse, fine], axis=1)
    zeros = jnp.zeros((N, C), jnp.bfloat16)
    ones = jnp.ones((N, C), jnp.bfloat16)
    head_keys, head_sources = [], []
    for head in range(H):
        lanes = head_lanes(N, head)
        picked = jnp.where(lanes, keys, zeros)
        head_keys.append(jnp.concatenate([picked, picked], axis=1))
        head_sources.append(
            jnp.concatenate([jnp.where(lanes, values, zeros), jnp.where(lanes, ones, zeros)], axis=1)
        )
    return both_queries, gating, head_keys, head_sources


def score(both_queries, head_keys):
    return lax.dot_general(
        both_queries, head_keys, CONTRACT_LAST, preferred_element_type=jnp.float32
    )


def softmax(scores, bias):
    scores = scores + bias
    highest = jnp.max(scores, axis=-1, keepdims=True)
    return jnp.exp2(scores - highest).astype(jnp.bfloat16)


def mix(head_weights, head_sources):
    return dot(jnp.concatenate(head_weights, axis=1), jnp.concatenate(head_sources, axis=0))


def finish(queries_in, summed, gating, w_out):
    hidden = (summed[:, :C] / summed[:, C:] * gating).astype(jnp.bfloat16)
    return (queries_in + dot(hidden, w_out)).astype(jnp.bfloat16).astype(jnp.float32)


def attend_rows(rows, bias_s, gain, w_query, w_key, w_value, w_gate, w_out):
    pre = [prepare(q, o, gain, w_query, w_key, w_value, w_gate) for q, o in rows]
    scores = [score(p[0], jnp.concatenate(p[2], axis=0)) for p in pre]
    summed = []
    for p, sc in zip(pre, scores):
        weights = [softmax(sc[:, h * N : (h + 1) * N], bias_s[h]) for h in range(H)]
        summed.append(mix(weights, p[3]))
    return [finish(q, m, p[1], w_out) for (q, o), m, p in zip(rows, summed, pre)]


def start_kernel(own_q, own_o, far_q, far_o, mask, gain, next_bias, *rest):
    weights, bias = rest[:2]
    out, tile, bias_s = rest[2:]

    @pl.when(pl.program_id(0) == 0)
    def _():
        for place in range(8):
            for head in range(H):
                for part in range(CHUNKS):
                    lanes = slice(part * C, (part + 1) * C)
                    bias_s[head, place * PART : (place + 1) * PART, lanes] = (
                        bias[place, head, part].astype(jnp.float32) * LOG2E + mask[:, lanes]
                    )

    afters = attend_rows(
        ((merged(own_q), merged(own_o)), (merged(far_q), merged(far_o))),
        bias_s,
        gain[0:1],
        *(weights[position] for position in range(5)),
    )
    for slot in range(2):
        after = afters[slot]
        out[:, 0, slot] = after.reshape(8, PART, C).astype(jnp.bfloat16)
        normed = normalize(after, gain[1:2])
        tile[slot, 0] = head_rows(next_bias[1], normed)


def end_kernel(own_q, own_o, far_q, far_o, mask, gain, *rest):
    weights, bias = rest[:2]
    out, bias_s, turned_s = rest[2:]

    @pl.when(pl.program_id(0) == 0)
    def _():
        row = lax.broadcasted_iota(jnp.int32, (HALF, 2 * HALF), 0)
        col = lax.broadcasted_iota(jnp.int32, (HALF, 2 * HALF), 1)
        for pair in range(2):
            for place in range(8):
                for side in range(2):
                    first = side * HALF + place * PART
                    for part in range(CHUNKS):
                        turned_s[pair, first : first + PART, part * C : (part + 1) * C] = bias[
                            place, pair, side, part
                        ].astype(jnp.float32)
        for head in range(H):
            chosen = jnp.where(row + (head % 2) * HALF == col, 1.0, 0.0).astype(jnp.bfloat16)
            turned = lax.dot_general(
                chosen,
                turned_s[head // 2].astype(jnp.bfloat16),
                CONTRACT_LAST,
                preferred_element_type=jnp.float32,
            )
            bias_s[head] = turned * LOG2E + mask[...]

    afters = attend_rows(
        ((merged(own_q), merged(own_o)), (merged(far_q), merged(far_o))),
        bias_s,
        gain[1:2],
        *(weights[position] for position in range(5)),
    )
    for slot in range(2):
        after = afters[slot]
        out[:, 0, slot] = after.reshape(8, PART, C).astype(jnp.bfloat16)


def head_rows(head_bias, normed):
    return lax.dot_general(
        head_bias, normed, (((0,), (1,)), ((), ())), preferred_element_type=jnp.float32
    )


def merged(block):
    return block[...].astype(jnp.float32).reshape(HALF, C)


def tile_kernel(block, gain, head_bias, *rest):
    weights, (tile, stacked) = rest[:5], rest[5:]

    @pl.when(pl.program_id(0) == 0)
    def _():
        for position, weight in enumerate(weights):
            stacked[:, position] = weight[...]

    tokens = block[...].astype(jnp.float32).reshape(8 * 2 * PART, C)
    normed = normalize(tokens, gain[0:1])
    tile[...] = head_rows(head_bias[0], normed)


def spread_kernel(arrived, spread):
    blocks = [
        jnp.concatenate([arrived[column, 2 * OWN + part].astype(jnp.float32) for part in range(3)], axis=1)
        for column in range(8)
    ]
    for head in range(H):
        lanes = []
        for side in range(2):
            first = (head * 2 + side) * PART
            lanes += [block[:, first : first + PART] for block in blocks]
        joined = jnp.concatenate(lanes, axis=1).astype(jnp.bfloat16)
        for part in range(CHUNKS):
            for copy in range(8):
                spread[copy, head, part] = joined[:, part * C : (part + 1) * C]


def whole(array):
    return pl.BlockSpec(array.shape, lambda *_: (0,) * array.ndim)


def attend(section, xa, xs, mask, gain, next_bias, weights, bias):
    first = pl.BlockSpec((8, None, PART, C), lambda step: (0, step, 0, 0))
    second = pl.BlockSpec((8, None, PART, C), lambda step: (0, OWN + step, 0, 0))
    weight = pl.BlockSpec((None, 5, C, C), lambda step: (section, 0, 0, 0))
    out_shape = [jax.ShapeDtypeStruct((8, OWN, 2, PART, C), jnp.bfloat16)]
    out_specs = [pl.BlockSpec((8, 1, 2, PART, C), lambda step: (0, step, 0, 0, 0))]
    scratch = [pltpu.VMEM((H, HALF, N), jnp.float32)]
    shared = [mask, gain]
    if section == 0:
        shared.append(next_bias)
        out_shape.append(jax.ShapeDtypeStruct((2, OWN, H, HALF), jnp.float32))
        out_specs.append(pl.BlockSpec((2, 1, H, HALF), lambda step: (0, step, 0, 0)))
    else:
        scratch.append(pltpu.VMEM((2, N, 2 * HALF), jnp.float32))
    return pl.pallas_call(
        (start_kernel, end_kernel)[section],
        grid=(OWN,),
        in_specs=[first, second, second, first]
        + [whole(member) for member in shared]
        + [weight, whole(bias)],
        out_specs=out_specs,
        scratch_shapes=scratch,
        out_shape=out_shape,
        compiler_params=pltpu.CompilerParams(vmem_limit_bytes=VMEM),
        cost_estimate=pl.CostEstimate(
            flops=8_000_000_000, bytes_accessed=6_000_000, transcendentals=8_000_000
        ),
        name=("start_node", "end_node")[section],
    )(xa, xa, xs, xs, *shared, weights, bias)


def by_core(array, axis, core):
    return jnp.where(core == 1, jnp.flip(array, axis), array)


def to_columns(array):
    flat = array.reshape(8, -1, C)
    return lax.all_to_all(flat, "col", 0, 0, tiled=True).reshape(array.shape)


def to_rows(array):
    flat = array.reshape(8, -1, C)
    flat = lax.all_to_all(flat, "row", 0, 0, axis_index_groups=SAME_CORE, tiled=True)
    return flat.reshape(array.shape)


def to_all(array):
    return lax.all_to_all(array, ("row", "col"), 0, 0, axis_index_groups=CORE_PLANES, tiled=True)


def copies(array):
    return jnp.broadcast_to(array[None], (8,) + array.shape)


def body(pair_input, token_mask, ln_gain, w_query, w_key, w_value, w_gate, w_bias, w_out):
    core = lax.axis_index("row") % 2
    mask_row = jnp.where(token_mask > 0, 0.0, masked_score).astype(jnp.float32)
    mask_row = by_core(mask_row.reshape(8, 2, PART), 1, core).transpose(1, 0, 2).reshape(1, N)
    weights = [w_query, w_key, w_value, w_gate, w_out]

    tile, weights = pl.pallas_call(
        tile_kernel,
        grid=(5,),
        in_specs=[
            pl.BlockSpec((8, 2 * PART, C), lambda step: (step, 0, 0)),
            whole(ln_gain),
            whole(w_bias),
        ]
        + [whole(weight) for weight in weights],
        out_specs=[
            pl.BlockSpec((H, 16 * PART), lambda step: (0, step)),
            pl.BlockSpec((2, 5, C, C), lambda step: (0, 0, 0, 0)),
        ],
        out_shape=[
            jax.ShapeDtypeStruct((H, 2 * PART * PART), jnp.float32),
            jax.ShapeDtypeStruct((2, 5, C, C), jnp.bfloat16),
        ],
        name="bias_tile",
    )(pair_input, ln_gain, w_bias, *weights)
    tile = by_core(tile.reshape(H, PART, 2, PART), 2, core).astype(jnp.bfloat16)
    tile = jnp.pad(
        tile.transpose(1, 0, 2, 3).reshape(PART, HALF), ((0, 0), (0, 3 * C - HALF))
    )
    tile = tile.reshape(PART, 3, C).transpose(1, 0, 2)
    halves = by_core(pair_input.reshape(8, OWN, 2, PART, C), 2, core)
    halves = halves.transpose(0, 2, 1, 3, 4).reshape(8, 2 * OWN, PART, C)
    xa = to_columns(jnp.concatenate([halves, copies(tile)], axis=1))
    xs = lax.ppermute(xa, "row", PARTNER)
    tile = pl.pallas_call(
        spread_kernel,
        grid=(1,),
        in_specs=[pl.BlockSpec((8, 13, PART, C), lambda step: (0, 0, 0, 0))],
        out_specs=pl.BlockSpec((8, H, CHUNKS, PART, C), lambda step: (0,) * 5),
        out_shape=jax.ShapeDtypeStruct((8, H, CHUNKS, PART, C), jnp.bfloat16),
        name="spread_tile",
    )(xa)
    bias = to_rows(tile)
    after, tile = attend(0, xa, xs, mask_row, ln_gain, w_bias, weights, bias)

    sent = after.reshape(8, OWN, 2, 8, OWN, C).transpose(3, 0, 2, 4, 1, 5)
    tile = tile.astype(jnp.bfloat16).reshape(2 * OWN, 2 * CHUNKS, C)
    tile = jnp.broadcast_to(
        tile.transpose(1, 0, 2).reshape(1, 100, C), (64, 100, C)
    )
    got = to_all(jnp.concatenate([sent.reshape(64, 2 * OWN * OWN, C), tile], axis=1))
    xa = got[:, : 2 * OWN * OWN].reshape(8, 8, 2 * OWN, OWN, C)
    xa = xa.transpose(0, 2, 1, 3, 4).reshape(8, 2 * OWN, PART, C)
    xs = lax.ppermute(xa, "row", PARTNER)
    bias = got[:, 2 * OWN * OWN :].reshape(8, 8, 2, CHUNKS, 2, OWN, C)
    bias = bias.transpose(0, 2, 4, 3, 1, 5, 6).reshape(8, 2, 2, CHUNKS, PART, C)
    (after,) = attend(1, xa, xs, mask_row, ln_gain, None, weights, bias)
    block = by_core(to_rows(after), 2, core)
    return block.transpose(3, 2, 0, 1, 4).reshape(PART, 2 * PART, C)


def solution(mesh):
    placed = (P("row", "col", None), P(), P(), P(), P(), P(), P(), P(), P())
    return jax.shard_map(
        body, mesh=mesh, in_specs=placed, out_specs=P("row", "col", None), check_vma=False
    )
```

```python
import functools

import jax
import jax.numpy as jnp
from jax import lax
from jax.experimental import pallas as pl
from jax.experimental.pallas import tpu as pltpu
from jax.sharding import PartitionSpec as P

H = 4
HD = 32
C = 128
N = 640
HALF = N // 2
PART = 40
OWN = 5

epsilon = 1e-05
masked_score = -1e30
LOG2E = 1.4426950408889634
SCALE = HD ** (-0.5) * LOG2E

SAME_CORE = [[core + 2 * place for place in range(8)] for core in range(2)]
CORE_PLANES = [
    [(core + 2 * place) * 8 + column for place in range(8) for column in range(8)]
    for core in range(2)
]
PARTNER = [(place, place ^ 1) for place in range(16)]

CHUNKS = N // C
VMEM = 30 * 1024 * 1024
CONTRACT_LAST = (((1,), (1,)), ((), ()))


def normalize(upcast, gain_row):
    centred = upcast - jnp.mean(upcast, axis=-1, keepdims=True)
    variance = jnp.mean(centred * centred, axis=-1, keepdims=True)
    return (centred * lax.rsqrt(variance + epsilon) * gain_row).astype(jnp.bfloat16)


def dot(left, right):
    return jnp.dot(left, right, preferred_element_type=jnp.float32)


def head_lanes(rows, head):
    lane = lax.broadcasted_iota(jnp.int32, (rows, C), 1)
    return (lane >= head * HD) & (lane < (head + 1) * HD)


def prepare(queries_in, others_in, gain, w_query, w_key, w_value, w_gate):
    own = normalize(queries_in, gain)
    other = normalize(others_in, gain)
    own_all = dot(own, jnp.concatenate([w_query, w_gate, w_key, w_value], axis=1))
    other_all = dot(other, jnp.concatenate([w_key, w_value], axis=1))
    queries = own_all[:, :C].astype(jnp.bfloat16).astype(jnp.float32) * SCALE
    gating = jax.nn.sigmoid(own_all[:, C : 2 * C])
    keys = jnp.concatenate([own_all[:, 2 * C : 3 * C], other_all[:, :C]], axis=0).astype(jnp.bfloat16)
    values = jnp.concatenate([own_all[:, 3 * C :], other_all[:, C:]], axis=0).astype(jnp.bfloat16)
    coarse = queries.astype(jnp.bfloat16)
    fine = (queries - coarse.astype(jnp.float32)).astype(jnp.bfloat16)
    both_queries = jnp.concatenate([coarse, fine], axis=1)
    zeros = jnp.zeros((N, C), jnp.bfloat16)
    ones = jnp.ones((N, C), jnp.bfloat16)
    head_keys, head_sources = [], []
    for head in range(H):
        lanes = head_lanes(N, head)
        picked = jnp.where(lanes, keys, zeros)
        head_keys.append(jnp.concatenate([picked, picked], axis=1))
        head_sources.append(
            jnp.concatenate([jnp.where(lanes, values, zeros), jnp.where(lanes, ones, zeros)], axis=1)
        )
    return both_queries, gating, head_keys, head_sources


def score(both_queries, head_keys):
    return lax.dot_general(
        both_queries, head_keys, CONTRACT_LAST, preferred_element_type=jnp.float32
    )


def softmax(scores, bias):
    scores = scores + bias
    highest = jnp.max(scores, axis=-1, keepdims=True)
    return jnp.exp2(scores - highest).astype(jnp.bfloat16)


def mix(head_weights, head_sources):
    return dot(jnp.concatenate(head_weights, axis=1), jnp.concatenate(head_sources, axis=0))


def finish(queries_in, summed, gating, w_out):
    hidden = (summed[:, :C] / summed[:, C:] * gating).astype(jnp.bfloat16)
    return (queries_in + dot(hidden, w_out)).astype(jnp.bfloat16).astype(jnp.float32)


def attend_rows(rows, bias_s, gain, w_query, w_key, w_value, w_gate, w_out):
    pre = [prepare(q, o, gain, w_query, w_key, w_value, w_gate) for q, o in rows]
    scores = [score(p[0], jnp.concatenate(p[2], axis=0)) for p in pre]
    summed = []
    for p, sc in zip(pre, scores):
        parts = []
        for first in (0, 160):
            piece = slice(first, first + 160)
            weights = [softmax(sc[piece, h * N : (h + 1) * N], bias_s[h, piece]) for h in range(H)]
            parts.append(mix(weights, p[3]))
        summed.append(jnp.concatenate(parts, axis=0))
    return [finish(q, m, p[1], w_out) for (q, o), m, p in zip(rows, summed, pre)]


def start_kernel(own_q, own_o, far_q, far_o, mask, gain, next_bias, *rest):
    weights, bias = rest[:2]
    out, tile, bias_s = rest[2:]

    @pl.when(pl.program_id(0) == 0)
    def _():
        for place in range(8):
            for head in range(H):
                for part in range(CHUNKS):
                    lanes = slice(part * C, (part + 1) * C)
                    bias_s[head, place * PART : (place + 1) * PART, lanes] = (
                        bias[place, head, part].astype(jnp.float32) * LOG2E + mask[:, lanes]
                    )

    afters = attend_rows(
        ((merged(own_q), merged(own_o)), (merged(far_q), merged(far_o))),
        bias_s,
        gain[0:1],
        *(weights[position] for position in range(5)),
    )
    for slot in range(2):
        after = afters[slot]
        out[:, 0, slot] = after.reshape(8, PART, C).astype(jnp.bfloat16)
        normed = normalize(after, gain[1:2])
        tile[slot, 0] = head_rows(next_bias[1], normed)


def end_kernel(own_q, own_o, far_q, far_o, mask, gain, *rest):
    weights, bias = rest[:2]
    out, bias_s, turned_s = rest[2:]

    @pl.when(pl.program_id(0) == 0)
    def _():
        row = lax.broadcasted_iota(jnp.int32, (HALF, 2 * HALF), 0)
        col = lax.broadcasted_iota(jnp.int32, (HALF, 2 * HALF), 1)
        for pair in range(2):
            for place in range(8):
                for side in range(2):
                    first = side * HALF + place * PART
                    for part in range(CHUNKS):
                        turned_s[pair, first : first + PART, part * C : (part + 1) * C] = bias[
                            place, pair, side, part
                        ].astype(jnp.float32)
        for head in range(H):
            chosen = jnp.where(row + (head % 2) * HALF == col, 1.0, 0.0).astype(jnp.bfloat16)
            turned = lax.dot_general(
                chosen,
                turned_s[head // 2].astype(jnp.bfloat16),
                CONTRACT_LAST,
                preferred_element_type=jnp.float32,
            )
            bias_s[head] = turned * LOG2E + mask[...]

    afters = attend_rows(
        ((merged(own_q), merged(own_o)), (merged(far_q), merged(far_o))),
        bias_s,
        gain[1:2],
        *(weights[position] for position in range(5)),
    )
    for slot in range(2):
        after = afters[slot]
        out[:, 0, slot] = after.reshape(8, PART, C).astype(jnp.bfloat16)


def head_rows(head_bias, normed):
    return lax.dot_general(head_bias, normed, CONTRACT_LAST, preferred_element_type=jnp.float32)


def merged(block):
    return block[...].astype(jnp.float32).reshape(HALF, C)


def tile_kernel(block, gain, head_bias, *rest):
    weights, (tile, stacked) = rest[:5], rest[5:]

    for position, weight in enumerate(weights):
        stacked[:, position] = weight[...]
    tokens = block[...].astype(jnp.float32).reshape(2 * PART * PART, C)
    normed = normalize(tokens, gain[0:1])
    tile[...] = head_rows(head_bias[0], normed)


def spread_kernel(arrived, spread):
    blocks = [
        jnp.concatenate([arrived[column, 2 * OWN + part].astype(jnp.float32) for part in range(3)], axis=1)
        for column in range(8)
    ]
    for head in range(H):
        lanes = []
        for side in range(2):
            first = (head * 2 + side) * PART
            lanes += [block[:, first : first + PART] for block in blocks]
        joined = jnp.concatenate(lanes, axis=1).astype(jnp.bfloat16)
        for part in range(CHUNKS):
            for copy in range(8):
                spread[copy, head, part] = joined[:, part * C : (part + 1) * C]


def whole(array):
    return pl.BlockSpec(array.shape, lambda *_: (0,) * array.ndim)


def attend(section, xa, xs, mask, gain, next_bias, weights, bias):
    first = pl.BlockSpec((8, None, PART, C), lambda step: (0, step, 0, 0))
    second = pl.BlockSpec((8, None, PART, C), lambda step: (0, OWN + step, 0, 0))
    weight = pl.BlockSpec((None, 5, C, C), lambda step: (section, 0, 0, 0))
    out_shape = [jax.ShapeDtypeStruct((8, OWN, 2, PART, C), jnp.bfloat16)]
    out_specs = [pl.BlockSpec((8, 1, 2, PART, C), lambda step: (0, step, 0, 0, 0))]
    scratch = [pltpu.VMEM((H, HALF, N), jnp.float32)]
    shared = [mask, gain]
    if section == 0:
        shared.append(next_bias)
        out_shape.append(jax.ShapeDtypeStruct((2, OWN, H, HALF), jnp.float32))
        out_specs.append(pl.BlockSpec((2, 1, H, HALF), lambda step: (0, step, 0, 0)))
    else:
        scratch.append(pltpu.VMEM((2, N, 2 * HALF), jnp.float32))
    return pl.pallas_call(
        (start_kernel, end_kernel)[section],
        grid=(OWN,),
        in_specs=[first, second, second, first]
        + [whole(member) for member in shared]
        + [weight, whole(bias)],
        out_specs=out_specs,
        scratch_shapes=scratch,
        out_shape=out_shape,
        compiler_params=pltpu.CompilerParams(vmem_limit_bytes=VMEM),
        cost_estimate=pl.CostEstimate(
            flops=8_000_000_000, bytes_accessed=6_000_000, transcendentals=8_000_000
        ),
        name=("start_node", "end_node")[section],
    )(xa, xa, xs, xs, *shared, weights, bias)


def by_core(array, axis, core):
    return jnp.where(core == 1, jnp.flip(array, axis), array)


def to_columns(array):
    flat = array.reshape(8, -1, C)
    return lax.all_to_all(flat, "col", 0, 0, tiled=True).reshape(array.shape)


def to_rows(array):
    flat = array.reshape(8, -1, C)
    flat = lax.all_to_all(flat, "row", 0, 0, axis_index_groups=SAME_CORE, tiled=True)
    return flat.reshape(array.shape)


def to_all(array):
    return lax.all_to_all(array, ("row", "col"), 0, 0, axis_index_groups=CORE_PLANES, tiled=True)


def copies(array):
    return jnp.broadcast_to(array[None], (8,) + array.shape)


def body(pair_input, token_mask, ln_gain, w_query, w_key, w_value, w_gate, w_bias, w_out):
    core = lax.axis_index("row") % 2
    mask_row = jnp.where(token_mask > 0, 0.0, masked_score).astype(jnp.float32)
    mask_row = by_core(mask_row.reshape(8, 2, PART), 1, core).transpose(1, 0, 2).reshape(1, N)
    head_bias = w_bias.transpose(0, 2, 1)
    weights = [w_query, w_key, w_value, w_gate, w_out]

    tile, weights = pl.pallas_call(
        tile_kernel,
        grid=(1,),
        in_specs=[whole(member) for member in (pair_input, ln_gain, head_bias, *weights)],
        out_specs=[
            pl.BlockSpec((H, 2 * PART * PART), lambda step: (0, 0)),
            pl.BlockSpec((2, 5, C, C), lambda step: (0, 0, 0, 0)),
        ],
        out_shape=[
            jax.ShapeDtypeStruct((H, 2 * PART * PART), jnp.float32),
            jax.ShapeDtypeStruct((2, 5, C, C), jnp.bfloat16),
        ],
        name="bias_tile",
    )(pair_input, ln_gain, head_bias, *weights)
    tile = by_core(tile.reshape(H, PART, 2, PART), 2, core).astype(jnp.bfloat16)
    tile = jnp.pad(
        tile.transpose(1, 0, 2, 3).reshape(PART, HALF), ((0, 0), (0, 3 * C - HALF))
    )
    tile = tile.reshape(PART, 3, C).transpose(1, 0, 2)
    halves = by_core(pair_input.reshape(8, OWN, 2, PART, C), 2, core)
    halves = halves.transpose(0, 2, 1, 3, 4).reshape(8, 2 * OWN, PART, C)
    xa = to_columns(jnp.concatenate([halves, copies(tile)], axis=1))
    xs = lax.ppermute(xa, "row", PARTNER)
    tile = pl.pallas_call(
        spread_kernel,
        grid=(1,),
        in_specs=[pl.BlockSpec((8, 13, PART, C), lambda step: (0, 0, 0, 0))],
        out_specs=pl.BlockSpec((8, H, CHUNKS, PART, C), lambda step: (0,) * 5),
        out_shape=jax.ShapeDtypeStruct((8, H, CHUNKS, PART, C), jnp.bfloat16),
        name="spread_tile",
    )(xa)
    bias = to_rows(tile)
    after, tile = attend(0, xa, xs, mask_row, ln_gain, head_bias, weights, bias)

    sent = after.reshape(8, OWN, 2, 8, OWN, C).transpose(3, 0, 2, 4, 1, 5)
    tile = tile.astype(jnp.bfloat16).reshape(2 * OWN, 2 * CHUNKS, C)
    tile = jnp.broadcast_to(
        tile.transpose(1, 0, 2).reshape(1, 100, C), (64, 100, C)
    )
    got = to_all(jnp.concatenate([sent.reshape(64, 2 * OWN * OWN, C), tile], axis=1))
    xa = got[:, : 2 * OWN * OWN].reshape(8, 8, 2 * OWN, OWN, C)
    xa = xa.transpose(0, 2, 1, 3, 4).reshape(8, 2 * OWN, PART, C)
    xs = lax.ppermute(xa, "row", PARTNER)
    bias = got[:, 2 * OWN * OWN :].reshape(8, 8, 2, CHUNKS, 2, OWN, C)
    bias = bias.transpose(0, 2, 4, 3, 1, 5, 6).reshape(8, 2, 2, CHUNKS, PART, C)
    (after,) = attend(1, xa, xs, mask_row, ln_gain, None, weights, bias)
    block = by_core(to_rows(after), 2, core)
    return block.transpose(3, 2, 0, 1, 4).reshape(PART, 2 * PART, C)


def solution(mesh):
    placed = (P("row", "col", None), P(), P(), P(), P(), P(), P(), P(), P())
    return jax.shard_map(
        body, mesh=mesh, in_specs=placed, out_specs=P("row", "col", None), check_vma=False
    )
```

```python
import functools

import jax
import jax.numpy as jnp
from jax import lax
from jax.experimental import pallas as pl
from jax.experimental.pallas import tpu as pltpu
from jax.sharding import PartitionSpec as P

H = 4
HD = 32
C = 128
N = 640
HALF = N // 2
PART = 40
OWN = 5

epsilon = 1e-05
masked_score = -1e30
LOG2E = 1.4426950408889634
SCALE = HD ** (-0.5) * LOG2E

SAME_CORE = [[core + 2 * place for place in range(8)] for core in range(2)]
CORE_PLANES = [
    [(core + 2 * place) * 8 + column for place in range(8) for column in range(8)]
    for core in range(2)
]
PARTNER = [(place, place ^ 1) for place in range(16)]

CHUNKS = N // C
VMEM = 30 * 1024 * 1024
CONTRACT_LAST = (((1,), (1,)), ((), ()))


def normalize(upcast, gain_row):
    centred = upcast - jnp.mean(upcast, axis=-1, keepdims=True)
    variance = jnp.mean(centred * centred, axis=-1, keepdims=True)
    return (centred * lax.rsqrt(variance + epsilon) * gain_row).astype(jnp.bfloat16)


def dot(left, right):
    return jnp.dot(left, right, preferred_element_type=jnp.float32)


def head_lanes(rows, head):
    lane = lax.broadcasted_iota(jnp.int32, (rows, C), 1)
    return (lane >= head * HD) & (lane < (head + 1) * HD)


def prepare(queries_in, others_in, gain, w_query, w_key, w_value, w_gate):
    own = normalize(queries_in, gain)
    other = normalize(others_in, gain)
    own_all = dot(own, jnp.concatenate([w_query, w_gate, w_key, w_value], axis=1))
    other_all = dot(other, jnp.concatenate([w_key, w_value], axis=1))
    queries = own_all[:, :C].astype(jnp.bfloat16).astype(jnp.float32) * SCALE
    gating = jax.nn.sigmoid(own_all[:, C : 2 * C])
    keys = jnp.concatenate([own_all[:, 2 * C : 3 * C], other_all[:, :C]], axis=0).astype(jnp.bfloat16)
    values = jnp.concatenate([own_all[:, 3 * C :], other_all[:, C:]], axis=0).astype(jnp.bfloat16)
    coarse = queries.astype(jnp.bfloat16)
    fine = (queries - coarse.astype(jnp.float32)).astype(jnp.bfloat16)
    both_queries = jnp.concatenate([coarse, fine], axis=1)
    zeros = jnp.zeros((N, C), jnp.bfloat16)
    ones = jnp.ones((N, C), jnp.bfloat16)
    head_keys, head_sources = [], []
    for head in range(H):
        lanes = head_lanes(N, head)
        picked = jnp.where(lanes, keys, zeros)
        head_keys.append(jnp.concatenate([picked, picked], axis=1))
        head_sources.append(
            jnp.concatenate([jnp.where(lanes, values, zeros), jnp.where(lanes, ones, zeros)], axis=1)
        )
    return both_queries, gating, head_keys, head_sources


def score(both_queries, head_keys):
    return lax.dot_general(
        both_queries, head_keys, CONTRACT_LAST, preferred_element_type=jnp.float32
    )


def softmax(scores, bias):
    scores = scores + bias
    highest = jnp.max(scores, axis=-1, keepdims=True)
    return jnp.exp2(scores - highest).astype(jnp.bfloat16)


def mix(head_weights, head_sources):
    return dot(jnp.concatenate(head_weights, axis=1), jnp.concatenate(head_sources, axis=0))


def finish(queries_in, summed, gating, w_out):
    hidden = (summed[:, :C] / summed[:, C:] * gating).astype(jnp.bfloat16)
    return (queries_in + dot(hidden, w_out)).astype(jnp.bfloat16).astype(jnp.float32)


def attend_rows(rows, bias_s, gain, w_query, w_key, w_value, w_gate, w_out):
    pre = [prepare(q, o, gain, w_query, w_key, w_value, w_gate) for q, o in rows]
    scores = [score(p[0], jnp.concatenate(p[2], axis=0)) for p in pre]
    summed = []
    for p, sc in zip(pre, scores):
        parts = []
        for first in (0, 160):
            piece = slice(first, first + 160)
            weights = [softmax(sc[piece, h * N : (h + 1) * N], bias_s[h, piece]) for h in range(H)]
            parts.append(mix(weights, p[3]))
        summed.append(jnp.concatenate(parts, axis=0))
    return [finish(q, m, p[1], w_out) for (q, o), m, p in zip(rows, summed, pre)]


def start_kernel(xa, xs, mask, gain, next_bias, *rest):
    weights, bias = rest[:2]
    out, tile, bias_s = rest[2:]

    for place in range(8):
        for head in range(H):
            for part in range(CHUNKS):
                lanes = slice(part * C, (part + 1) * C)
                bias_s[head, place * PART : (place + 1) * PART, lanes] = (
                    bias[place, head, part].astype(jnp.float32) * LOG2E + mask[:, lanes]
                )

    def pair(step):
        afters = attend_rows(
            row_pair(xa, xs, step),
            bias_s,
            gain[0:1],
            *(weights[0, position] for position in range(5)),
        )
        for slot in range(2):
            after = afters[slot]
            out[:, step, slot] = after.reshape(8, PART, C).astype(jnp.bfloat16)
            normed = normalize(after, gain[1:2])
            tile[slot, step] = head_rows(next_bias[1], normed)

    pair(0)
    pl.loop(1, OWN)(pair)


def end_kernel(xa, xs, mask, gain, *rest):
    weights, bias = rest[:2]
    out, bias_s, turned_s = rest[2:]

    row = lax.broadcasted_iota(jnp.int32, (HALF, 2 * HALF), 0)
    col = lax.broadcasted_iota(jnp.int32, (HALF, 2 * HALF), 1)
    for pair in range(2):
        for place in range(8):
            for side in range(2):
                first = side * HALF + place * PART
                for part in range(CHUNKS):
                    turned_s[pair, first : first + PART, part * C : (part + 1) * C] = bias[
                        place, pair, side, part
                    ].astype(jnp.float32)
    for head in range(H):
        chosen = jnp.where(row + (head % 2) * HALF == col, 1.0, 0.0).astype(jnp.bfloat16)
        turned = lax.dot_general(
            chosen,
            turned_s[head // 2].astype(jnp.bfloat16),
            CONTRACT_LAST,
            preferred_element_type=jnp.float32,
        )
        bias_s[head] = turned * LOG2E + mask[...]

    def pair(step):
        afters = attend_rows(
            row_pair(xa, xs, step),
            bias_s,
            gain[1:2],
            *(weights[1, position] for position in range(5)),
        )
        for slot in range(2):
            after = afters[slot]
            out[:, step, slot] = after.reshape(8, PART, C).astype(jnp.bfloat16)

    pair(0)
    pl.loop(1, OWN)(pair)


def head_rows(head_bias, normed):
    return lax.dot_general(head_bias, normed, CONTRACT_LAST, preferred_element_type=jnp.float32)


def row_pair(xa, xs, step):
    own = [xa[:, position].astype(jnp.float32).reshape(HALF, C) for position in (step, OWN + step)]
    far = [xs[:, position].astype(jnp.float32).reshape(HALF, C) for position in (OWN + step, step)]
    return own, far


def open_kernel(core, block, gain, head_bias, *rest):
    weights, (send, stacked, tile_s) = rest[:5], rest[5:]
    for position, weight in enumerate(weights):
        stacked[:, position] = weight[...]
    tokens = block[...].astype(jnp.float32)
    swapped = core[0] == 1
    low, high = tokens[:, :PART], tokens[:, PART:]
    halves = [jnp.where(swapped, high, low), jnp.where(swapped, low, high)]
    for column in range(8):
        for side in range(2):
            for row in range(OWN):
                send[column, side * OWN + row] = halves[side][column * OWN + row].astype(jnp.bfloat16)
    normed = normalize(jnp.concatenate(halves, axis=1).reshape(2 * PART * PART, C), gain[0:1])
    by_head = head_rows(head_bias[0], normed)
    tile_s[...] = jnp.zeros_like(tile_s)
    for row in range(PART):
        for head in range(H):
            tile_s[row : row + 1, head * 2 * PART : (head + 1) * 2 * PART] = by_head[
                head : head + 1, row * 2 * PART : (row + 1) * 2 * PART
            ]
    for part in range(3):
        lanes = tile_s[:, part * C : (part + 1) * C].astype(jnp.bfloat16)
        for column in range(8):
            send[column, 2 * OWN + part] = lanes


def spread_kernel(arrived, spread):
    blocks = [
        jnp.concatenate([arrived[column, 2 * OWN + part].astype(jnp.float32) for part in range(3)], axis=1)
        for column in range(8)
    ]
    for head in range(H):
        lanes = []
        for side in range(2):
            first = (head * 2 + side) * PART
            lanes += [block[:, first : first + PART] for block in blocks]
        joined = jnp.concatenate(lanes, axis=1).astype(jnp.bfloat16)
        for part in range(CHUNKS):
            for copy in range(8):
                spread[copy, head, part] = joined[:, part * C : (part + 1) * C]


def whole(array):
    return pl.BlockSpec(array.shape, lambda *_: (0,) * array.ndim)


def attend(section, xa, xs, mask, gain, next_bias, weights, bias):
    out_shape = [jax.ShapeDtypeStruct((8, OWN, 2, PART, C), jnp.bfloat16)]
    scratch = [pltpu.VMEM((H, HALF, N), jnp.float32)]
    operands = [xa, xs, mask, gain]
    if section == 0:
        operands.append(next_bias)
        out_shape.append(jax.ShapeDtypeStruct((2, OWN, H, HALF), jnp.float32))
    else:
        scratch.append(pltpu.VMEM((2, N, 2 * HALF), jnp.float32))
    operands += [weights, bias]
    resident = pl.BlockSpec(memory_space=pltpu.VMEM)
    return pl.pallas_call(
        (start_kernel, end_kernel)[section],
        in_specs=[resident] * len(operands),
        out_specs=[resident] * len(out_shape),
        scratch_shapes=scratch,
        out_shape=out_shape,
        compiler_params=pltpu.CompilerParams(vmem_limit_bytes=VMEM),
        cost_estimate=pl.CostEstimate(
            flops=8_000_000_000, bytes_accessed=6_000_000, transcendentals=8_000_000
        ),
        name=("start_node", "end_node")[section],
    )(*operands)


def by_core(array, axis, core):
    return jnp.where(core == 1, jnp.flip(array, axis), array)


def to_columns(array):
    flat = array.reshape(8, -1, C)
    return lax.all_to_all(flat, "col", 0, 0, tiled=True).reshape(array.shape)


def to_rows(array):
    flat = array.reshape(8, -1, C)
    flat = lax.all_to_all(flat, "row", 0, 0, axis_index_groups=SAME_CORE, tiled=True)
    return flat.reshape(array.shape)


def to_all(array):
    return lax.all_to_all(array, ("row", "col"), 0, 0, axis_index_groups=CORE_PLANES, tiled=True)


def copies(array):
    return jnp.broadcast_to(array[None], (8,) + array.shape)


def body(pair_input, token_mask, ln_gain, w_query, w_key, w_value, w_gate, w_bias, w_out):
    core = lax.axis_index("row") % 2
    mask_row = jnp.where(token_mask > 0, 0.0, masked_score).astype(jnp.float32)
    mask_row = by_core(mask_row.reshape(8, 2, PART), 1, core).transpose(1, 0, 2).reshape(1, N)
    head_bias = w_bias.transpose(0, 2, 1)
    weights = [w_query, w_key, w_value, w_gate, w_out]

    resident = pl.BlockSpec(memory_space=pltpu.VMEM)
    sent, weights = pl.pallas_call(
        open_kernel,
        in_specs=[pl.BlockSpec(memory_space=pltpu.SMEM)] + [resident] * 8,
        out_specs=[resident] * 2,
        out_shape=[
            jax.ShapeDtypeStruct((8, 2 * OWN + 3, PART, C), jnp.bfloat16),
            jax.ShapeDtypeStruct((2, 5, C, C), jnp.bfloat16),
        ],
        scratch_shapes=[pltpu.VMEM((PART, 3 * C), jnp.float32)],
        name="open",
    )(core.reshape(1).astype(jnp.int32), pair_input, ln_gain, head_bias, *weights)
    xa = to_columns(sent)
    xs = lax.ppermute(xa, "row", PARTNER)
    tile = pl.pallas_call(
        spread_kernel,
        in_specs=[pl.BlockSpec(memory_space=pltpu.VMEM)],
        out_specs=pl.BlockSpec(memory_space=pltpu.VMEM),
        out_shape=jax.ShapeDtypeStruct((8, H, CHUNKS, PART, C), jnp.bfloat16),
        name="spread_tile",
    )(xa)
    bias = to_rows(tile)
    after, tile = attend(0, xa, xs, mask_row, ln_gain, head_bias, weights, bias)

    sent = after.reshape(8, OWN, 2, 8, OWN, C).transpose(3, 0, 2, 4, 1, 5)
    tile = tile.astype(jnp.bfloat16).reshape(2 * OWN, 2 * CHUNKS, C)
    tile = jnp.broadcast_to(
        tile.transpose(1, 0, 2).reshape(1, 100, C), (64, 100, C)
    )
    got = to_all(jnp.concatenate([sent.reshape(64, 2 * OWN * OWN, C), tile], axis=1))
    xa = got[:, : 2 * OWN * OWN].reshape(8, 8, 2 * OWN, OWN, C)
    xa = xa.transpose(0, 2, 1, 3, 4).reshape(8, 2 * OWN, PART, C)
    xs = lax.ppermute(xa, "row", PARTNER)
    bias = got[:, 2 * OWN * OWN :].reshape(8, 8, 2, CHUNKS, 2, OWN, C)
    bias = bias.transpose(0, 2, 4, 3, 1, 5, 6).reshape(8, 2, 2, CHUNKS, PART, C)
    (after,) = attend(1, xa, xs, mask_row, ln_gain, None, weights, bias)
    block = by_core(to_rows(after), 2, core)
    return block.transpose(3, 2, 0, 1, 4).reshape(PART, 2 * PART, C)


def solution(mesh):
    placed = (P("row", "col", None), P(), P(), P(), P(), P(), P(), P(), P())
    return jax.shard_map(
        body, mesh=mesh, in_specs=placed, out_specs=P("row", "col", None), check_vma=False
    )
```

```python
import functools

import jax
import jax.numpy as jnp
from jax import lax
from jax.experimental import pallas as pl
from jax.experimental.pallas import tpu as pltpu
from jax.sharding import PartitionSpec as P

H = 4
HD = 32
C = 128
N = 640
HALF = N // 2
PART = 40
OWN = 5

epsilon = 1e-05
masked_score = -1e30
LOG2E = 1.4426950408889634
SCALE = HD ** (-0.5) * LOG2E

SAME_CORE = [[core + 2 * place for place in range(8)] for core in range(2)]
CORE_PLANES = [
    [(core + 2 * place) * 8 + column for place in range(8) for column in range(8)]
    for core in range(2)
]
PARTNER = [(place, place ^ 1) for place in range(16)]

CHUNKS = N // C
VMEM = 30 * 1024 * 1024
CONTRACT_LAST = (((1,), (1,)), ((), ()))


def normalize(upcast, gain_row):
    centred = upcast - jnp.mean(upcast, axis=-1, keepdims=True)
    variance = jnp.mean(centred * centred, axis=-1, keepdims=True)
    return (centred * lax.rsqrt(variance + epsilon) * gain_row).astype(jnp.bfloat16)


def dot(left, right):
    return jnp.dot(left, right, preferred_element_type=jnp.float32)


def head_lanes(rows, head):
    lane = lax.broadcasted_iota(jnp.int32, (rows, C), 1)
    return (lane >= head * HD) & (lane < (head + 1) * HD)


def prepare(queries_in, others_in, gain, w_query, w_key, w_value, w_gate):
    own = normalize(queries_in, gain)
    other = normalize(others_in, gain)
    own_all = dot(own, jnp.concatenate([w_query, w_gate, w_key, w_value], axis=1))
    other_all = dot(other, jnp.concatenate([w_key, w_value], axis=1))
    queries = own_all[:, :C].astype(jnp.bfloat16).astype(jnp.float32) * SCALE
    gating = jax.nn.sigmoid(own_all[:, C : 2 * C])
    keys = jnp.concatenate([own_all[:, 2 * C : 3 * C], other_all[:, :C]], axis=0).astype(jnp.bfloat16)
    values = jnp.concatenate([own_all[:, 3 * C :], other_all[:, C:]], axis=0).astype(jnp.bfloat16)
    coarse = queries.astype(jnp.bfloat16)
    fine = (queries - coarse.astype(jnp.float32)).astype(jnp.bfloat16)
    both_queries = jnp.concatenate([coarse, fine], axis=1)
    zeros = jnp.zeros((N, C), jnp.bfloat16)
    ones = jnp.ones((N, C), jnp.bfloat16)
    head_keys, head_sources = [], []
    for head in range(H):
        lanes = head_lanes(N, head)
        picked = jnp.where(lanes, keys, zeros)
        head_keys.append(jnp.concatenate([picked, picked], axis=1))
        head_sources.append(
            jnp.concatenate([jnp.where(lanes, values, zeros), jnp.where(lanes, ones, zeros)], axis=1)
        )
    return both_queries, gating, head_keys, head_sources


def score(both_queries, head_keys):
    return lax.dot_general(
        both_queries, head_keys, CONTRACT_LAST, preferred_element_type=jnp.float32
    )


def softmax(scores, bias):
    scores = scores + bias
    highest = jnp.max(scores, axis=-1, keepdims=True)
    return jnp.exp2(scores - highest).astype(jnp.bfloat16)


def mix(head_weights, head_sources):
    return dot(jnp.concatenate(head_weights, axis=1), jnp.concatenate(head_sources, axis=0))


def finish(queries_in, summed, gating, w_out):
    hidden = (summed[:, :C] / summed[:, C:] * gating).astype(jnp.bfloat16)
    return (queries_in + dot(hidden, w_out)).astype(jnp.bfloat16).astype(jnp.float32)


def attend_rows(rows, bias_s, gain, w_query, w_key, w_value, w_gate, w_out):
    pre = [prepare(q, o, gain, w_query, w_key, w_value, w_gate) for q, o in rows]
    scores = [score(p[0], jnp.concatenate(p[2], axis=0)) for p in pre]
    summed = []
    for p, sc in zip(pre, scores):
        parts = []
        for first in (0, 160):
            piece = slice(first, first + 160)
            weights = [softmax(sc[piece, h * N : (h + 1) * N], bias_s[h, piece]) for h in range(H)]
            parts.append(mix(weights, p[3]))
        summed.append(jnp.concatenate(parts, axis=0))
    return [finish(q, m, p[1], w_out) for (q, o), m, p in zip(rows, summed, pre)]


def start_kernel(xa, xs, mask, gain, next_bias, *rest):
    weights, bias = rest[:2]
    out, tile, bias_s = rest[2:]

    for place in range(8):
        for head in range(H):
            for part in range(CHUNKS):
                lanes = slice(part * C, (part + 1) * C)
                bias_s[head, place * PART : (place + 1) * PART, lanes] = (
                    bias[place, head, part].astype(jnp.float32) * LOG2E + mask[:, lanes]
                )

    def pair(step):
        afters = attend_rows(
            row_pair(xa, xs, step),
            bias_s,
            gain[0:1],
            *(weights[0, position] for position in range(5)),
        )
        for slot in range(2):
            after = afters[slot]
            out[:, step, slot] = after.reshape(8, PART, C).astype(jnp.bfloat16)
            normed = normalize(after, gain[1:2])
            tile[slot, step] = head_rows(next_bias[1], normed)

    pair(0)
    pl.loop(1, OWN)(pair)


def end_kernel(xa, xs, mask, gain, *rest):
    weights, bias = rest[:2]
    out, bias_s, turned_s = rest[2:]

    for pair in range(2):
        for place in range(8):
            for side in range(2):
                first = side * HALF + place * PART
                for part in range(CHUNKS):
                    turned_s[pair, first : first + PART, part * C : (part + 1) * C] = bias[
                        place, pair, side, part
                    ].astype(jnp.float32)
    for head in range(H):
        first = (head % 2) * HALF
        turned = turned_s[head // 2, :, first : first + HALF].T
        bias_s[head] = turned * LOG2E + mask[...]

    def pair(step):
        afters = attend_rows(
            row_pair(xa, xs, step),
            bias_s,
            gain[1:2],
            *(weights[1, position] for position in range(5)),
        )
        for slot in range(2):
            after = afters[slot]
            out[:, step, slot] = after.reshape(8, PART, C).astype(jnp.bfloat16)

    pair(0)
    pl.loop(1, OWN)(pair)


def head_rows(head_bias, normed):
    return lax.dot_general(head_bias, normed, CONTRACT_LAST, preferred_element_type=jnp.float32)


def row_pair(xa, xs, step):
    own = [xa[:, position].astype(jnp.float32).reshape(HALF, C) for position in (step, OWN + step)]
    far = [xs[:, position].astype(jnp.float32).reshape(HALF, C) for position in (OWN + step, step)]
    return own, far


def open_kernel(core, block, gain, head_bias, *rest):
    weights, (send, stacked, tile_s) = rest[:5], rest[5:]
    for position, weight in enumerate(weights):
        stacked[:, position] = weight[...]
    tokens = block[...].astype(jnp.float32)
    swapped = core[0] == 1
    low, high = tokens[:, :PART], tokens[:, PART:]
    halves = [jnp.where(swapped, high, low), jnp.where(swapped, low, high)]
    for column in range(8):
        for side in range(2):
            for row in range(OWN):
                send[column, side * OWN + row] = halves[side][column * OWN + row].astype(jnp.bfloat16)
    normed = normalize(jnp.concatenate(halves, axis=1).reshape(2 * PART * PART, C), gain[0:1])
    by_head = head_rows(head_bias[0], normed)
    tile_s[...] = jnp.zeros_like(tile_s)
    for row in range(PART):
        for head in range(H):
            tile_s[row : row + 1, head * 2 * PART : (head + 1) * 2 * PART] = by_head[
                head : head + 1, row * 2 * PART : (row + 1) * 2 * PART
            ]
    for part in range(3):
        lanes = tile_s[:, part * C : (part + 1) * C].astype(jnp.bfloat16)
        for column in range(8):
            send[column, 2 * OWN + part] = lanes


def spread_kernel(arrived, spread):
    blocks = [
        jnp.concatenate([arrived[column, 2 * OWN + part].astype(jnp.float32) for part in range(3)], axis=1)
        for column in range(8)
    ]
    for head in range(H):
        lanes = []
        for side in range(2):
            first = (head * 2 + side) * PART
            lanes += [block[:, first : first + PART] for block in blocks]
        joined = jnp.concatenate(lanes, axis=1).astype(jnp.bfloat16)
        for part in range(CHUNKS):
            for copy in range(8):
                spread[copy, head, part] = joined[:, part * C : (part + 1) * C]


def whole(array):
    return pl.BlockSpec(array.shape, lambda *_: (0,) * array.ndim)


def attend(section, xa, xs, mask, gain, next_bias, weights, bias):
    out_shape = [jax.ShapeDtypeStruct((8, OWN, 2, PART, C), jnp.bfloat16)]
    scratch = [pltpu.VMEM((H, HALF, N), jnp.float32)]
    operands = [xa, xs, mask, gain]
    if section == 0:
        operands.append(next_bias)
        out_shape.append(jax.ShapeDtypeStruct((2, OWN, H, HALF), jnp.float32))
    else:
        scratch.append(pltpu.VMEM((2, N, 2 * HALF), jnp.float32))
    operands += [weights, bias]
    resident = pl.BlockSpec(memory_space=pltpu.VMEM)
    return pl.pallas_call(
        (start_kernel, end_kernel)[section],
        in_specs=[resident] * len(operands),
        out_specs=[resident] * len(out_shape),
        scratch_shapes=scratch,
        out_shape=out_shape,
        compiler_params=pltpu.CompilerParams(vmem_limit_bytes=VMEM),
        cost_estimate=pl.CostEstimate(
            flops=8_000_000_000, bytes_accessed=6_000_000, transcendentals=8_000_000
        ),
        name=("start_node", "end_node")[section],
    )(*operands)


def by_core(array, axis, core):
    return jnp.where(core == 1, jnp.flip(array, axis), array)


def to_columns(array):
    flat = array.reshape(8, -1, C)
    return lax.all_to_all(flat, "col", 0, 0, tiled=True).reshape(array.shape)


def to_rows(array):
    flat = array.reshape(8, -1, C)
    flat = lax.all_to_all(flat, "row", 0, 0, axis_index_groups=SAME_CORE, tiled=True)
    return flat.reshape(array.shape)


def to_all(array):
    return lax.all_to_all(array, ("row", "col"), 0, 0, axis_index_groups=CORE_PLANES, tiled=True)


def copies(array):
    return jnp.broadcast_to(array[None], (8,) + array.shape)


def body(pair_input, token_mask, ln_gain, w_query, w_key, w_value, w_gate, w_bias, w_out):
    core = lax.axis_index("row") % 2
    mask_row = jnp.where(token_mask > 0, 0.0, masked_score).astype(jnp.float32)
    mask_row = by_core(mask_row.reshape(8, 2, PART), 1, core).transpose(1, 0, 2).reshape(1, N)
    head_bias = w_bias.transpose(0, 2, 1)
    weights = [w_query, w_key, w_value, w_gate, w_out]

    resident = pl.BlockSpec(memory_space=pltpu.VMEM)
    sent, weights = pl.pallas_call(
        open_kernel,
        in_specs=[pl.BlockSpec(memory_space=pltpu.SMEM)] + [resident] * 8,
        out_specs=[resident] * 2,
        out_shape=[
            jax.ShapeDtypeStruct((8, 2 * OWN + 3, PART, C), jnp.bfloat16),
            jax.ShapeDtypeStruct((2, 5, C, C), jnp.bfloat16),
        ],
        scratch_shapes=[pltpu.VMEM((PART, 3 * C), jnp.float32)],
        name="open",
    )(core.reshape(1).astype(jnp.int32), pair_input, ln_gain, head_bias, *weights)
    xa = to_columns(sent)
    xs = lax.ppermute(xa, "row", PARTNER)
    tile = pl.pallas_call(
        spread_kernel,
        in_specs=[pl.BlockSpec(memory_space=pltpu.VMEM)],
        out_specs=pl.BlockSpec(memory_space=pltpu.VMEM),
        out_shape=jax.ShapeDtypeStruct((8, H, CHUNKS, PART, C), jnp.bfloat16),
        name="spread_tile",
    )(xa)
    bias = to_rows(tile)
    after, tile = attend(0, xa, xs, mask_row, ln_gain, head_bias, weights, bias)

    sent = after.reshape(8, OWN, 2, 8, OWN, C).transpose(3, 0, 2, 4, 1, 5)
    tile = tile.astype(jnp.bfloat16).reshape(2 * OWN, 2 * CHUNKS, C)
    tile = jnp.broadcast_to(
        tile.transpose(1, 0, 2).reshape(1, 100, C), (64, 100, C)
    )
    got = to_all(jnp.concatenate([sent.reshape(64, 2 * OWN * OWN, C), tile], axis=1))
    xa = got[:, : 2 * OWN * OWN].reshape(8, 8, 2 * OWN, OWN, C)
    xa = xa.transpose(0, 2, 1, 3, 4).reshape(8, 2 * OWN, PART, C)
    xs = lax.ppermute(xa, "row", PARTNER)
    bias = got[:, 2 * OWN * OWN :].reshape(8, 8, 2, CHUNKS, 2, OWN, C)
    bias = bias.transpose(0, 2, 4, 3, 1, 5, 6).reshape(8, 2, 2, CHUNKS, PART, C)
    (after,) = attend(1, xa, xs, mask_row, ln_gain, None, weights, bias)
    block = by_core(to_rows(after), 2, core)
    return block.transpose(3, 2, 0, 1, 4).reshape(PART, 2 * PART, C)


def solution(mesh):
    placed = (P("row", "col", None), P(), P(), P(), P(), P(), P(), P(), P())
    return jax.shard_map(
        body, mesh=mesh, in_specs=placed, out_specs=P("row", "col", None), check_vma=False
    )
```

```python
import functools

import jax
import jax.numpy as jnp
from jax import lax
from jax.experimental import pallas as pl
from jax.experimental.pallas import tpu as pltpu
from jax.sharding import PartitionSpec as P

H = 4
HD = 32
C = 128
N = 640
HALF = N // 2
PART = 40
OWN = 5

epsilon = 1e-05
masked_score = -1e30
LOG2E = 1.4426950408889634
SCALE = HD ** (-0.5) * LOG2E

SAME_CORE = [[core + 2 * place for place in range(8)] for core in range(2)]
CORE_PLANES = [
    [(core + 2 * place) * 8 + column for place in range(8) for column in range(8)]
    for core in range(2)
]
PARTNER = [(place, place ^ 1) for place in range(16)]

CHUNKS = N // C
VMEM = 30 * 1024 * 1024
CONTRACT_LAST = (((1,), (1,)), ((), ()))


def normalize(upcast, gain_row):
    centred = upcast - jnp.mean(upcast, axis=-1, keepdims=True)
    variance = jnp.mean(centred * centred, axis=-1, keepdims=True)
    return (centred * lax.rsqrt(variance + epsilon) * gain_row).astype(jnp.bfloat16)


def dot(left, right):
    return jnp.dot(left, right, preferred_element_type=jnp.float32)


def head_lanes(rows, head):
    lane = lax.broadcasted_iota(jnp.int32, (rows, C), 1)
    return (lane >= head * HD) & (lane < (head + 1) * HD)


def prepare(queries_in, others_in, gain, w_query, w_key, w_value, w_gate):
    normed = normalize(jnp.concatenate([queries_in, others_in], axis=0), gain)
    own_all = dot(normed[:HALF], jnp.concatenate([w_query, w_gate], axis=1))
    both = dot(normed, jnp.concatenate([w_key, w_value], axis=1)).astype(jnp.bfloat16)
    keys, values = both[:, :C], both[:, C:]
    queries = own_all[:, :C].astype(jnp.bfloat16).astype(jnp.float32) * SCALE
    gating = jax.nn.sigmoid(own_all[:, C : 2 * C])
    coarse = queries.astype(jnp.bfloat16)
    fine = (queries - coarse.astype(jnp.float32)).astype(jnp.bfloat16)
    both_queries = jnp.concatenate([coarse, fine], axis=1)
    zeros = jnp.zeros((N, C), jnp.bfloat16)
    ones = jnp.ones((N, C), jnp.bfloat16)
    head_keys, head_sources = [], []
    for head in range(H):
        lanes = head_lanes(N, head)
        picked = jnp.where(lanes, keys, zeros)
        head_keys.append(jnp.concatenate([picked, picked], axis=1))
        head_sources.append(
            jnp.concatenate([jnp.where(lanes, values, zeros), jnp.where(lanes, ones, zeros)], axis=1)
        )
    return both_queries, gating, head_keys, head_sources


def score(both_queries, head_keys):
    return lax.dot_general(
        both_queries, head_keys, CONTRACT_LAST, preferred_element_type=jnp.float32
    )


def softmax(scores, bias):
    scores = scores + bias
    highest = jnp.max(scores, axis=-1, keepdims=True)
    return jnp.exp2(scores - highest).astype(jnp.bfloat16)


def mix(head_weights, head_sources):
    return dot(jnp.concatenate(head_weights, axis=1), jnp.concatenate(head_sources, axis=0))


def finish(queries_in, summed, gating, w_out):
    hidden = (summed[:, :C] / summed[:, C:] * gating).astype(jnp.bfloat16)
    return (queries_in + dot(hidden, w_out)).astype(jnp.bfloat16).astype(jnp.float32)


def attend_rows(rows, bias_s, gain, w_query, w_key, w_value, w_gate, w_out):
    pre = [prepare(q, o, gain, w_query, w_key, w_value, w_gate) for q, o in rows]
    scores = [score(p[0], jnp.concatenate(p[2], axis=0)) for p in pre]
    summed = []
    for p, sc in zip(pre, scores):
        parts = []
        for first in (0, 160):
            piece = slice(first, first + 160)
            weights = [softmax(sc[piece, h * N : (h + 1) * N], bias_s[h, piece]) for h in range(H)]
            parts.append(mix(weights, p[3]))
        summed.append(jnp.concatenate(parts, axis=0))
    return [finish(q, m, p[1], w_out) for (q, o), m, p in zip(rows, summed, pre)]


def start_kernel(xa, xs, mask, gain, next_bias, *rest):
    weights, bias = rest[:2]
    out, tile, bias_s = rest[2:]

    for place in range(8):
        for head in range(H):
            for part in range(CHUNKS):
                lanes = slice(part * C, (part + 1) * C)
                bias_s[head, place * PART : (place + 1) * PART, lanes] = (
                    bias[place, head, part].astype(jnp.float32) * LOG2E + mask[:, lanes]
                )

    def pair(step):
        afters = attend_rows(
            row_pair(xa, xs, step),
            bias_s,
            gain[0:1],
            *(weights[0, position] for position in range(5)),
        )
        for slot in range(2):
            after = afters[slot]
            out[:, step, slot] = after.reshape(8, PART, C).astype(jnp.bfloat16)
        normed = normalize(jnp.concatenate(afters, axis=0), gain[1:2])
        tile[step] = head_rows(next_bias[1], normed)

    pair(0)
    pl.loop(1, OWN)(pair)


def end_kernel(xa, xs, mask, gain, *rest):
    weights, bias = rest[:2]
    out, bias_s, turned_s = rest[2:]

    for pair in range(2):
        for place in range(8):
            for side in range(2):
                first = side * HALF + place * PART
                for part in range(CHUNKS):
                    turned_s[pair, first : first + PART, part * C : (part + 1) * C] = bias[
                        place, pair, side, part
                    ].astype(jnp.float32)
    for head in range(H):
        first = (head % 2) * HALF
        turned = turned_s[head // 2, :, first : first + HALF].T
        bias_s[head] = turned * LOG2E + mask[...]

    def pair(step):
        afters = attend_rows(
            row_pair(xa, xs, step),
            bias_s,
            gain[1:2],
            *(weights[1, position] for position in range(5)),
        )
        for slot in range(2):
            after = afters[slot]
            out[:, step, slot] = after.reshape(8, PART, C).astype(jnp.bfloat16)

    pair(0)
    pl.loop(1, OWN)(pair)


def head_rows(head_bias, normed):
    return lax.dot_general(head_bias, normed, CONTRACT_LAST, preferred_element_type=jnp.float32)


def row_pair(xa, xs, step):
    own = [xa[:, position].astype(jnp.float32).reshape(HALF, C) for position in (step, OWN + step)]
    far = [xs[:, position].astype(jnp.float32).reshape(HALF, C) for position in (OWN + step, step)]
    return own, far


def open_kernel(core, block, gain, head_bias, *rest):
    weights, (send, stacked, tile_s) = rest[:5], rest[5:]
    for position, weight in enumerate(weights):
        stacked[:, position] = weight[...]
    tokens = block[...].astype(jnp.float32)
    swapped = core[0] == 1
    low, high = tokens[:, :PART], tokens[:, PART:]
    halves = [jnp.where(swapped, high, low), jnp.where(swapped, low, high)]
    for column in range(8):
        for side in range(2):
            for row in range(OWN):
                send[column, side * OWN + row] = halves[side][column * OWN + row].astype(jnp.bfloat16)
    normed = normalize(jnp.concatenate(halves, axis=1).reshape(2 * PART * PART, C), gain[0:1])
    by_head = head_rows(head_bias[0], normed)
    tile_s[...] = jnp.zeros_like(tile_s)
    for row in range(PART):
        for head in range(H):
            tile_s[row : row + 1, head * 2 * PART : (head + 1) * 2 * PART] = by_head[
                head : head + 1, row * 2 * PART : (row + 1) * 2 * PART
            ]
    for part in range(3):
        lanes = tile_s[:, part * C : (part + 1) * C].astype(jnp.bfloat16)
        for column in range(8):
            send[column, 2 * OWN + part] = lanes


def spread_kernel(arrived, spread):
    blocks = [
        jnp.concatenate([arrived[column, 2 * OWN + part].astype(jnp.float32) for part in range(3)], axis=1)
        for column in range(8)
    ]
    for head in range(H):
        lanes = []
        for side in range(2):
            first = (head * 2 + side) * PART
            lanes += [block[:, first : first + PART] for block in blocks]
        joined = jnp.concatenate(lanes, axis=1).astype(jnp.bfloat16)
        for part in range(CHUNKS):
            for copy in range(8):
                spread[copy, head, part] = joined[:, part * C : (part + 1) * C]


def whole(array):
    return pl.BlockSpec(array.shape, lambda *_: (0,) * array.ndim)


def attend(section, xa, xs, mask, gain, next_bias, weights, bias):
    out_shape = [jax.ShapeDtypeStruct((8, OWN, 2, PART, C), jnp.bfloat16)]
    scratch = [pltpu.VMEM((H, HALF, N), jnp.float32)]
    operands = [xa, xs, mask, gain]
    if section == 0:
        operands.append(next_bias)
        out_shape.append(jax.ShapeDtypeStruct((OWN, H, 2 * HALF), jnp.float32))
    else:
        scratch.append(pltpu.VMEM((2, N, 2 * HALF), jnp.float32))
    operands += [weights, bias]
    resident = pl.BlockSpec(memory_space=pltpu.VMEM)
    return pl.pallas_call(
        (start_kernel, end_kernel)[section],
        in_specs=[resident] * len(operands),
        out_specs=[resident] * len(out_shape),
        scratch_shapes=scratch,
        out_shape=out_shape,
        compiler_params=pltpu.CompilerParams(vmem_limit_bytes=VMEM),
        cost_estimate=pl.CostEstimate(
            flops=8_000_000_000, bytes_accessed=6_000_000, transcendentals=8_000_000
        ),
        name=("start_node", "end_node")[section],
    )(*operands)


def by_core(array, axis, core):
    return jnp.where(core == 1, jnp.flip(array, axis), array)


def to_columns(array):
    flat = array.reshape(8, -1, C)
    return lax.all_to_all(flat, "col", 0, 0, tiled=True).reshape(array.shape)


def to_rows(array):
    flat = array.reshape(8, -1, C)
    flat = lax.all_to_all(flat, "row", 0, 0, axis_index_groups=SAME_CORE, tiled=True)
    return flat.reshape(array.shape)


def to_all(array):
    return lax.all_to_all(array, ("row", "col"), 0, 0, axis_index_groups=CORE_PLANES, tiled=True)


def copies(array):
    return jnp.broadcast_to(array[None], (8,) + array.shape)


def body(pair_input, token_mask, ln_gain, w_query, w_key, w_value, w_gate, w_bias, w_out):
    core = lax.axis_index("row") % 2
    mask_row = jnp.where(token_mask > 0, 0.0, masked_score).astype(jnp.float32)
    mask_row = by_core(mask_row.reshape(8, 2, PART), 1, core).transpose(1, 0, 2).reshape(1, N)
    head_bias = w_bias.transpose(0, 2, 1)
    weights = [w_query, w_key, w_value, w_gate, w_out]

    resident = pl.BlockSpec(memory_space=pltpu.VMEM)
    sent, weights = pl.pallas_call(
        open_kernel,
        in_specs=[pl.BlockSpec(memory_space=pltpu.SMEM)] + [resident] * 8,
        out_specs=[resident] * 2,
        out_shape=[
            jax.ShapeDtypeStruct((8, 2 * OWN + 3, PART, C), jnp.bfloat16),
            jax.ShapeDtypeStruct((2, 5, C, C), jnp.bfloat16),
        ],
        scratch_shapes=[pltpu.VMEM((PART, 3 * C), jnp.float32)],
        name="open",
    )(core.reshape(1).astype(jnp.int32), pair_input, ln_gain, head_bias, *weights)
    xa = to_columns(sent)
    xs = lax.ppermute(xa, "row", PARTNER)
    tile = pl.pallas_call(
        spread_kernel,
        in_specs=[pl.BlockSpec(memory_space=pltpu.VMEM)],
        out_specs=pl.BlockSpec(memory_space=pltpu.VMEM),
        out_shape=jax.ShapeDtypeStruct((8, H, CHUNKS, PART, C), jnp.bfloat16),
        name="spread_tile",
    )(xa)
    bias = to_rows(tile)
    after, tile = attend(0, xa, xs, mask_row, ln_gain, head_bias, weights, bias)

    sent = after.reshape(8, OWN, 2, 8, OWN, C).transpose(3, 0, 2, 4, 1, 5)
    tile = tile.astype(jnp.bfloat16).reshape(OWN, H, 2, HALF).transpose(2, 0, 1, 3)
    tile = tile.reshape(2 * OWN, 2 * CHUNKS, C)
    tile = jnp.broadcast_to(
        tile.transpose(1, 0, 2).reshape(1, 100, C), (64, 100, C)
    )
    got = to_all(jnp.concatenate([sent.reshape(64, 2 * OWN * OWN, C), tile], axis=1))
    xa = got[:, : 2 * OWN * OWN].reshape(8, 8, 2 * OWN, OWN, C)
    xa = xa.transpose(0, 2, 1, 3, 4).reshape(8, 2 * OWN, PART, C)
    xs = lax.ppermute(xa, "row", PARTNER)
    bias = got[:, 2 * OWN * OWN :].reshape(8, 8, 2, CHUNKS, 2, OWN, C)
    bias = bias.transpose(0, 2, 4, 3, 1, 5, 6).reshape(8, 2, 2, CHUNKS, PART, C)
    (after,) = attend(1, xa, xs, mask_row, ln_gain, None, weights, bias)
    block = by_core(to_rows(after), 2, core)
    return block.transpose(3, 2, 0, 1, 4).reshape(PART, 2 * PART, C)


def solution(mesh):
    placed = (P("row", "col", None), P(), P(), P(), P(), P(), P(), P(), P())
    return jax.shard_map(
        body, mesh=mesh, in_specs=placed, out_specs=P("row", "col", None), check_vma=False
    )
```

```python
import functools

import jax
import jax.numpy as jnp
from jax import lax
from jax.experimental import pallas as pl
from jax.experimental.pallas import tpu as pltpu
from jax.sharding import PartitionSpec as P

H = 4
HD = 32
C = 128
N = 640
HALF = N // 2
PART = 40
OWN = 5

epsilon = 1e-05
masked_score = -1e30
LOG2E = 1.4426950408889634
SCALE = HD ** (-0.5) * LOG2E

SAME_CORE = [[core + 2 * place for place in range(8)] for core in range(2)]
CORE_PLANES = [
    [(core + 2 * place) * 8 + column for place in range(8) for column in range(8)]
    for core in range(2)
]
PARTNER = [(place, place ^ 1) for place in range(16)]

CHUNKS = N // C
VMEM = 30 * 1024 * 1024
CONTRACT_LAST = (((1,), (1,)), ((), ()))


def normalize(upcast, gain_row):
    centred = upcast - jnp.mean(upcast, axis=-1, keepdims=True)
    variance = jnp.mean(centred * centred, axis=-1, keepdims=True)
    return (centred * lax.rsqrt(variance + epsilon) * gain_row).astype(jnp.bfloat16)


def dot(left, right):
    return jnp.dot(left, right, preferred_element_type=jnp.float32)


def head_lanes(rows, head):
    lane = lax.broadcasted_iota(jnp.int32, (rows, C), 1)
    return (lane >= head * HD) & (lane < (head + 1) * HD)


def prepare(queries_in, others_in, gain, w_query, w_key, w_value, w_gate):
    own = normalize(queries_in, gain)
    other = normalize(others_in, gain)
    own_all = dot(own, jnp.concatenate([w_query, w_gate, w_key, w_value], axis=1))
    other_all = dot(other, jnp.concatenate([w_key, w_value], axis=1))
    queries = own_all[:, :C].astype(jnp.bfloat16).astype(jnp.float32) * SCALE
    gating = jax.nn.sigmoid(own_all[:, C : 2 * C])
    keys = jnp.concatenate([own_all[:, 2 * C : 3 * C], other_all[:, :C]], axis=0).astype(jnp.bfloat16)
    values = jnp.concatenate([own_all[:, 3 * C :], other_all[:, C:]], axis=0).astype(jnp.bfloat16)
    coarse = queries.astype(jnp.bfloat16)
    fine = (queries - coarse.astype(jnp.float32)).astype(jnp.bfloat16)
    both_queries = jnp.concatenate([coarse, fine], axis=1)
    zeros = jnp.zeros((N, C), jnp.bfloat16)
    ones = jnp.ones((N, C), jnp.bfloat16)
    head_keys, head_sources = [], []
    for head in range(H):
        lanes = head_lanes(N, head)
        picked = jnp.where(lanes, keys, zeros)
        head_keys.append(jnp.concatenate([picked, picked], axis=1))
        head_sources.append(
            jnp.concatenate([jnp.where(lanes, values, zeros), jnp.where(lanes, ones, zeros)], axis=1)
        )
    return both_queries, gating, head_keys, head_sources


def score(both_queries, head_keys):
    return lax.dot_general(
        both_queries, head_keys, CONTRACT_LAST, preferred_element_type=jnp.float32
    )


def softmax(scores, bias):
    scores = scores + bias
    highest = jnp.max(scores, axis=-1, keepdims=True)
    return jnp.exp2(scores - highest).astype(jnp.bfloat16)


def mix(head_weights, head_sources):
    return dot(jnp.concatenate(head_weights, axis=1), jnp.concatenate(head_sources, axis=0))


def finish(queries_in, summed, gating, w_out):
    hidden = (summed[:, :C] / summed[:, C:] * gating).astype(jnp.bfloat16)
    return (queries_in + dot(hidden, w_out)).astype(jnp.bfloat16).astype(jnp.float32)


def attend_rows(rows, bias_s, gain, w_query, w_key, w_value, w_gate, w_out):
    pre = [prepare(q, o, gain, w_query, w_key, w_value, w_gate) for q, o in rows]
    scores = [score(p[0], jnp.concatenate(p[2], axis=0)) for p in pre]
    summed = []
    for p, sc in zip(pre, scores):
        parts = []
        for first in (0, 160):
            piece = slice(first, first + 160)
            weights = [softmax(sc[piece, h * N : (h + 1) * N], bias_s[h, piece]) for h in range(H)]
            parts.append(mix(weights, p[3]))
        summed.append(jnp.concatenate(parts, axis=0))
    return [finish(q, m, p[1], w_out) for (q, o), m, p in zip(rows, summed, pre)]


def start_kernel(xa, xs, mask, gain, next_bias, *rest):
    weights, bias = rest[:2]
    out, tile, bias_s = rest[2:]

    for place in range(8):
        for head in range(H):
            for part in range(CHUNKS):
                lanes = slice(part * C, (part + 1) * C)
                bias_s[head, place * PART : (place + 1) * PART, lanes] = (
                    bias[place, head, part].astype(jnp.float32) * LOG2E + mask[:, lanes]
                )

    def pair(step):
        afters = attend_rows(
            row_pair(xa, xs, step),
            bias_s,
            gain[0:1],
            *(weights[0, position] for position in range(5)),
        )
        for slot in range(2):
            after = afters[slot]
            out[:, step, slot] = after.reshape(8, PART, C).astype(jnp.bfloat16)
            normed = normalize(after, gain[1:2])
            tile[slot, step] = head_rows(next_bias[1], normed)

    pair(0)
    pl.loop(1, OWN)(pair)


def end_kernel(xa, xs, mask, gain, *rest):
    weights, bias = rest[:2]
    out, bias_s, turned_s = rest[2:]

    for pair in range(2):
        for place in range(8):
            for side in range(2):
                first = side * HALF + place * PART
                for part in range(CHUNKS):
                    turned_s[pair, first : first + PART, part * C : (part + 1) * C] = bias[
                        place, pair, side, part
                    ].astype(jnp.float32)
    for head in range(H):
        first = (head % 2) * HALF
        turned = turned_s[head // 2, :, first : first + HALF].T
        bias_s[head] = turned * LOG2E + mask[...]

    def pair(step):
        afters = attend_rows(
            row_pair(xa, xs, step),
            bias_s,
            gain[1:2],
            *(weights[1, position] for position in range(5)),
        )
        for slot in range(2):
            after = afters[slot]
            out[:, step, slot] = after.reshape(8, PART, C).astype(jnp.bfloat16)

    pair(0)
    pl.loop(1, OWN)(pair)


def head_rows(head_bias, normed):
    return lax.dot_general(head_bias, normed, CONTRACT_LAST, preferred_element_type=jnp.float32)


def row_pair(xa, xs, step):
    own = [xa[:, position].astype(jnp.float32).reshape(HALF, C) for position in (step, OWN + step)]
    far = [xs[:, position].astype(jnp.float32).reshape(HALF, C) for position in (OWN + step, step)]
    return own, far


def open_kernel(core, block, gain, head_bias, *rest):
    weights, (send, stacked, tile_s) = rest[:5], rest[5:]
    for position, weight in enumerate(weights):
        stacked[:, position] = weight[...]
    tokens = block[...].astype(jnp.float32)
    swapped = core[0] == 1
    low, high = tokens[:, :PART], tokens[:, PART:]
    halves = [jnp.where(swapped, high, low), jnp.where(swapped, low, high)]
    for column in range(8):
        for side in range(2):
            for row in range(OWN):
                send[column, side * OWN + row] = halves[side][column * OWN + row].astype(jnp.bfloat16)
    normed = normalize(jnp.concatenate(halves, axis=1).reshape(2 * PART * PART, C), gain[0:1])
    by_head = head_rows(head_bias[0], normed)
    tile_s[...] = jnp.zeros_like(tile_s)
    for row in range(PART):
        for head in range(H):
            tile_s[row : row + 1, head * 2 * PART : (head + 1) * 2 * PART] = by_head[
                head : head + 1, row * 2 * PART : (row + 1) * 2 * PART
            ]
    for part in range(3):
        lanes = tile_s[:, part * C : (part + 1) * C].astype(jnp.bfloat16)
        for column in range(8):
            send[column, 2 * OWN + part] = lanes


def spread_kernel(arrived, spread):
    blocks = [
        jnp.concatenate([arrived[column, 2 * OWN + part].astype(jnp.float32) for part in range(3)], axis=1)
        for column in range(8)
    ]
    for head in range(H):
        lanes = []
        for side in range(2):
            first = (head * 2 + side) * PART
            lanes += [block[:, first : first + PART] for block in blocks]
        joined = jnp.concatenate(lanes, axis=1).astype(jnp.bfloat16)
        for part in range(CHUNKS):
            for copy in range(8):
                spread[copy, head, part] = joined[:, part * C : (part + 1) * C]


def whole(array):
    return pl.BlockSpec(array.shape, lambda *_: (0,) * array.ndim)


def attend(section, xa, xs, mask, gain, next_bias, weights, bias):
    out_shape = [jax.ShapeDtypeStruct((8, OWN, 2, PART, C), jnp.bfloat16)]
    scratch = [pltpu.VMEM((H, HALF, N), jnp.float32)]
    operands = [xa, xs, mask, gain]
    if section == 0:
        operands.append(next_bias)
        out_shape.append(jax.ShapeDtypeStruct((2, OWN, H, HALF), jnp.float32))
    else:
        scratch.append(pltpu.VMEM((2, N, 2 * HALF), jnp.float32))
    operands += [weights, bias]
    resident = pl.BlockSpec(memory_space=pltpu.VMEM)
    return pl.pallas_call(
        (start_kernel, end_kernel)[section],
        in_specs=[resident] * len(operands),
        out_specs=[resident] * len(out_shape),
        scratch_shapes=scratch,
        out_shape=out_shape,
        compiler_params=pltpu.CompilerParams(vmem_limit_bytes=VMEM),
        cost_estimate=pl.CostEstimate(
            flops=8_000_000_000, bytes_accessed=6_000_000, transcendentals=8_000_000
        ),
        name=("start_node", "end_node")[section],
    )(*operands)


def by_core(array, axis, core):
    return jnp.where(core == 1, jnp.flip(array, axis), array)


def to_columns(array):
    flat = array.reshape(8, -1, C)
    return lax.all_to_all(flat, "col", 0, 0, tiled=True).reshape(array.shape)


def to_rows(array):
    flat = array.reshape(8, -1, C)
    flat = lax.all_to_all(flat, "row", 0, 0, axis_index_groups=SAME_CORE, tiled=True)
    return flat.reshape(array.shape)


def to_all(array):
    return lax.all_to_all(array, ("row", "col"), 0, 0, axis_index_groups=CORE_PLANES, tiled=True)


def copies(array):
    return jnp.broadcast_to(array[None], (8,) + array.shape)


def body(pair_input, token_mask, ln_gain, w_query, w_key, w_value, w_gate, w_bias, w_out):
    core = lax.axis_index("row") % 2
    mask_row = jnp.where(token_mask > 0, 0.0, masked_score).astype(jnp.float32)
    mask_row = by_core(mask_row.reshape(8, 2, PART), 1, core).transpose(1, 0, 2).reshape(1, N)
    head_bias = w_bias.transpose(0, 2, 1)
    weights = [w_query, w_key, w_value, w_gate, w_out]

    resident = pl.BlockSpec(memory_space=pltpu.VMEM)
    sent, weights = pl.pallas_call(
        open_kernel,
        in_specs=[pl.BlockSpec(memory_space=pltpu.SMEM)] + [resident] * 8,
        out_specs=[resident] * 2,
        out_shape=[
            jax.ShapeDtypeStruct((8, 2 * OWN + 3, PART, C), jnp.bfloat16),
            jax.ShapeDtypeStruct((2, 5, C, C), jnp.bfloat16),
        ],
        scratch_shapes=[pltpu.VMEM((PART, 3 * C), jnp.float32)],
        name="open",
    )(core.reshape(1).astype(jnp.int32), pair_input, ln_gain, head_bias, *weights)
    xa = to_columns(sent)
    xs = lax.ppermute(xa, "row", PARTNER)
    tile = pl.pallas_call(
        spread_kernel,
        in_specs=[pl.BlockSpec(memory_space=pltpu.VMEM)],
        out_specs=pl.BlockSpec(memory_space=pltpu.VMEM),
        out_shape=jax.ShapeDtypeStruct((8, H, CHUNKS, PART, C), jnp.bfloat16),
        name="spread_tile",
    )(xa)
    bias = to_rows(tile)
    after, tile = attend(0, xa, xs, mask_row, ln_gain, head_bias, weights, bias)

    sent = after.reshape(8, OWN, 2, 8, OWN, C).transpose(3, 0, 2, 4, 1, 5)
    tile = tile.astype(jnp.bfloat16).reshape(2 * OWN, 2 * CHUNKS, C)
    tile = jnp.broadcast_to(
        tile.transpose(1, 0, 2).reshape(1, 100, C), (64, 100, C)
    )
    got = to_all(jnp.concatenate([tile, sent.reshape(64, 2 * OWN * OWN, C)], axis=1))
    xa = got[:, 100:].reshape(8, 8, 2 * OWN, OWN, C)
    xa = xa.transpose(0, 2, 1, 3, 4).reshape(8, 2 * OWN, PART, C)
    xs = lax.ppermute(xa, "row", PARTNER)
    bias = got[:, :100].reshape(8, 8, 2, CHUNKS, 2, OWN, C)
    bias = bias.transpose(0, 2, 4, 3, 1, 5, 6).reshape(8, 2, 2, CHUNKS, PART, C)
    (after,) = attend(1, xa, xs, mask_row, ln_gain, None, weights, bias)
    block = by_core(to_rows(after), 2, core)
    return block.transpose(3, 2, 0, 1, 4).reshape(PART, 2 * PART, C)


def solution(mesh):
    placed = (P("row", "col", None), P(), P(), P(), P(), P(), P(), P(), P())
    return jax.shard_map(
        body, mesh=mesh, in_specs=placed, out_specs=P("row", "col", None), check_vma=False
    )
```
